128 devices in a mesh: dp: 8 (over z, y_lo), mp: 16 (over y_hi, x, core).
Axes of the slice: x: 4, y: 4 (y_hi: 2, y_lo: 2; y = y_hi * 2 + y_lo), z: 4, core: 2. Of those that a mesh axis runs over, the one named last changes fastest.
Arguments:
- tokens: bfloat16 [1024, 8192], P(('dp', 'mp')), may hold values from -6 to 6
- out_grad: bfloat16 [1024, 8192], P(('dp', 'mp')), may hold values from -6 to 6
- gate_pre: bfloat16 [1024, 24576], P(None, 'mp'), may hold values from -8 to 8
- up_pre: bfloat16 [1024, 24576], P(None, 'mp'), may hold values from -6 to 6
- gate_weight: bfloat16 [8192, 24576], P('dp', 'mp'), may hold values from -0.0625 to 0.0625
- up_weight: bfloat16 [8192, 24576], P('dp', 'mp'), may hold values from -0.0625 to 0.0625
- down_weight: bfloat16 [24576, 8192], P('mp', 'dp'), may hold values from -0.0390625 to 0.0390625
- lengths: int32 [8], P('dp'), may hold values from 1 to 128, as said below
Outputs:
- grad_tokens: bfloat16 [1024, 8192], P(('dp', 'mp'))
- grad_gate: bfloat16 [8192, 24576], P('dp', 'mp')
- grad_up: bfloat16 [8192, 24576], P('dp', 'mp')
- grad_down: bfloat16 [24576, 8192], P('mp', 'dp')
The draws below stay inside these ranges and needn't reach their ends.
Inputs may be any that keep to these rules, and one draw needn't show every extreme that they name: lengths count live rows from the start of each response's block of 128 rows; some response fills its block.
All inputs are finite; a program needn't handle non-finite values.
Results may differ from the reference program's by a relative error of at most 0.0051.
Values may be sent and summed in bfloat16 or wider, within the bound.
A program may use at most 128 MiB of HBM per device.

```python
import jax
import jax.numpy as jnp

D = 8192
FF = 24576
SEQ_LEN = 128
TOKENS = 1024
SEQS = 8


def draw_lengths(key, part):
    key = jax.random.fold_in(key, 11)
    first_key, second_key, third_key = jax.random.split(key, 3)
    first = jax.random.randint(first_key, (SEQS,), 1, SEQ_LEN + 1)
    second = jax.random.randint(second_key, (SEQS,), 1, SEQ_LEN + 1)
    chosen = jnp.minimum(first, second)
    where = jax.random.randint(third_key, (), 0, SEQS)
    return chosen.at[where].set(SEQ_LEN).astype(jnp.int32)


def steps_of(own_key, dims, cuts, least, top_value):
    loudness = 1.0
    for axis_at, shards_of in cuts:
        heights = jax.random.uniform(jax.random.fold_in(jax.random.fold_in(own_key, 6), axis_at), (shards_of,), jnp.float32, least / len(cuts), top_value / len(cuts))
        loudness = loudness * jnp.repeat(jnp.exp(heights), dims[axis_at] // shards_of).reshape((-1,) + (1,) * (len(dims) - 1 - axis_at))
    return loudness


def centred(key, dims, spread, reach, pieces=(), kind=jnp.bfloat16):
    array = jax.random.normal(key, dims, jnp.float32) * spread
    if len(pieces) > 0:
        array = steps_of(key, dims, pieces, -0.22, 0.18) * array
    return jnp.clip(array, min=-reach, max=reach).astype(kind)


def setup_inputs(seed: int = 0) -> dict:
    streams_of = jax.random.split(jax.random.key(seed), 9)
    tokens = centred(streams_of[0], (TOKENS, D), 1.0, 6.0, ((0, 128),))
    out_grad = centred(streams_of[1], (TOKENS, D), 1.0, 6.0, ((0, 128),))
    gate_pre = centred(streams_of[2], (TOKENS, FF), 1.5, 8.0, ((1, 16),))
    up_pre = centred(streams_of[3], (TOKENS, FF), 1.0, 6.0, ((1, 16),))
    gate_weight = centred(streams_of[4], (D, FF), D ** -0.5, 0.0625, ((0, 8), (1, 16)))
    up_weight = centred(streams_of[5], (D, FF), D ** -0.5, 0.0625, ((0, 8), (1, 16)))
    down_weight = centred(streams_of[6], (FF, D), FF ** -0.5, 0.0390625, ((0, 16), (1, 8)))
    lengths = draw_lengths(jax.random.fold_in(streams_of[8], 71), 0)
    return {"tokens": tokens, "out_grad": out_grad, "gate_pre": gate_pre, "up_pre": up_pre, "gate_weight": gate_weight, "up_weight": up_weight, "down_weight": down_weight, "lengths": lengths}


def gate_backward(dh, gate_f, up_f):
    sig = jax.nn.sigmoid(gate_f)
    dgate = (dh * up_f * sig * (1.0 + gate_f * (1.0 - sig))).astype(jnp.bfloat16)
    dup = (dh * gate_f * sig).astype(jnp.bfloat16)
    return dgate, dup


def reference(tokens, out_grad, gate_pre, up_pre, gate_weight, up_weight, down_weight, lengths):
    position = jnp.arange(TOKENS, dtype=jnp.int32)
    row_len = lengths[(position // SEQ_LEN).astype(jnp.int32)]
    live = (position % SEQ_LEN) < row_len
    masked = jnp.where(live[:, None], out_grad, jnp.zeros_like(out_grad))
    gate_f = gate_pre.astype(jnp.float32)
    up_f = up_pre.astype(jnp.float32)
    hidden = (gate_f * jax.nn.sigmoid(gate_f) * up_f).astype(jnp.bfloat16)
    dh = jnp.dot(masked, down_weight.T, preferred_element_type=jnp.float32)
    dgate, dup = gate_backward(dh, gate_f, up_f)
    grad_gate = jnp.dot(tokens.T, dgate, preferred_element_type=jnp.float32).astype(jnp.bfloat16)
    grad_up = jnp.dot(tokens.T, dup, preferred_element_type=jnp.float32).astype(jnp.bfloat16)
    grad_down = jnp.dot(hidden.T, masked, preferred_element_type=jnp.float32).astype(jnp.bfloat16)
    part_gate = jnp.dot(dgate, gate_weight.T, preferred_element_type=jnp.float32)
    part_up = jnp.dot(dup, up_weight.T, preferred_element_type=jnp.float32)
    grad_tokens = (part_gate + part_up).astype(jnp.bfloat16)
    return grad_tokens, grad_gate, grad_up, grad_down
```

```python
import functools

import jax
import jax.numpy as jnp
from jax import lax
from jax.experimental import pallas as pl
from jax.experimental.pallas import tpu as pltpu
from jax.sharding import PartitionSpec as P

SEQ_LEN = 128
NZ, NY = 4, 2
NF = 3
ND = 2
SIZES = (384, 512, 640, 1024)
BF, F32 = jnp.bfloat16, jnp.float32
MIB = 1 << 20

DP_TREE = (
    ((2, 1), (2, 0)),
    ((1, 1), (0, 1)),
    ((3, 1), (0, 1)),
    ((3, 0), (0, 0)),
    ((2, 0), (1, 0)),
    ((0, 1), (0, 0)),
    ((1, 0), (0, 0)),
)
MP_TREE = (
    ((2, 1), (1, 1)),
    ((3, 1), (0, 1)),
    ((2, 0), (1, 0)),
    ((3, 0), (0, 0)),
    ((1, 1), (0, 1)),
    ((1, 0), (0, 0)),
    ((0, 1), (0, 0)),
)


class Place:
    def __init__(self):
        self.dp = lax.axis_index("dp")
        self.mp = lax.axis_index("mp")
        self.z, self.yl = self.dp // NY, self.dp % NY
        self.core = self.mp % 2
        self.chip = self.mp // 2
        self.yh, self.x = self.chip // 4, self.chip % 4
        self.sign = 1 - 2 * self.core

    def dp_at(self, da, db):
        z = lax.rem(self.z + self.sign * da + 4, 4)
        return z * NY + (1 - self.yl if db else self.yl)

    def chip_at(self, da, db):
        x = lax.rem(self.x + self.sign * da + 4, 4)
        return (1 - self.yh if db else self.yh) * 4 + x

    def dp_hop(self, src, dst):
        return {"dp": self.dp_at(dst[0] - src[0], src[1] ^ dst[1])}

    def mp_hop(self, src, dst):
        return {"mp": self.chip_at(dst[0] - src[0], src[1] ^ dst[1]) * 2 + self.core}

    def sibling(self):
        return {"mp": self.chip * 2 + 1 - self.core}

    def barrier(self):
        sem = pltpu.get_barrier_semaphore()
        peers = [{"dp": lax.rem(self.dp + k, 8)} for k in range(1, 8)]
        peers += [self.sibling()]
        peers += [{"mp": self.chip_at(a, b) * 2 + self.core} for a, b in ((1, 0), (3, 0), (0, 1))]
        for peer in peers:
            pl.semaphore_signal(sem, inc=1, device_id=peer, device_id_type=pl.DeviceIdType.MESH)
        pl.semaphore_wait(sem, len(peers))


def send(src, dst, send_sem, recv_sem, device):
    copy = pltpu.make_async_remote_copy(
        src_ref=src,
        dst_ref=dst,
        send_sem=send_sem,
        recv_sem=recv_sem,
        device_id=device,
        device_id_type=pl.DeviceIdType.MESH,
    )
    copy.start()
    return copy


def dot_nt(a, b):
    return lax.dot_general(a, b, (((1,), (1,)), ((), ())), preferred_element_type=F32)


def dot(a, b):
    return jnp.dot(a, b, preferred_element_type=F32)


class Gather:
    EDGES = (
        ((0, 0), (0, 1)),
        ((0, 0), (1, 0)),
        ((0, 0), (3, 0)),
        ((0, 1), (1, 1)),
        ((0, 1), (3, 1)),
        ((1, 0), (2, 0)),
        ((1, 1), (2, 1)),
    )

    def __init__(self, at, buf, rows, sems, sib_sems):
        self.at, self.buf, self.rows = at, buf, rows
        self.send_sem, self.recv_sem = sems
        self.sib_send, self.sib_recv = sib_sems
        self.copies = []

    def slab(self, chip, core):
        start = pl.multiple_of((core * 8 + chip) * self.rows, self.rows)
        return self.buf.at[pl.ds(start, self.rows), :]

    def slab_from(self, offset):
        a, b = offset
        return self.slab(self.at.chip_at(-a, b), self.at.core)

    def to_sibling(self, n, offset):
        ref = self.slab_from(offset)
        self.copies.append(
            send(ref, ref, self.sib_send.at[n], self.sib_recv.at[n], self.at.sibling())
        )

    def hop(self, e):
        src, dst = self.EDGES[e]
        ref = self.slab_from(src)
        self.copies.append(
            send(ref, ref, self.send_sem.at[e], self.recv_sem.at[e], self.at.mp_hop(src, dst))
        )

    def arrive(self, e):
        _, dst = self.EDGES[e]
        ref = self.slab_from(dst)
        pltpu.make_async_remote_copy(
            src_ref=ref,
            dst_ref=ref,
            send_sem=self.send_sem.at[e],
            recv_sem=self.recv_sem.at[e],
            device_id=self.at.sibling(),
            device_id_type=pl.DeviceIdType.MESH,
        ).wait_recv()

    def stage(self, n):
        if n == 0:
            for e in (0, 1, 2):
                self.hop(e)
            self.to_sibling(7, (0, 0))
        elif n == 1:
            self.arrive(0)
            self.hop(3)
            self.hop(4)
            self.arrive(1)
            self.hop(5)
            self.to_sibling(0, (0, 1))
            self.to_sibling(1, (1, 0))
        elif n == 2:
            self.arrive(2)
            self.to_sibling(2, (3, 0))
            self.arrive(3)
            self.hop(6)
            self.to_sibling(3, (1, 1))
        elif n == 3:
            for e in (4, 5, 6):
                self.arrive(e)
                self.to_sibling(e, self.EDGES[e][1])
        else:
            for n, offset in enumerate([d for _, d in self.EDGES] + [(0, 0)]):
                a, b = offset
                chip = self.at.chip_at(a, b)
                ref = self.slab(chip, 1 - self.at.core)
                pltpu.make_async_remote_copy(
                    src_ref=ref,
                    dst_ref=ref,
                    send_sem=self.sib_send.at[n],
                    recv_sem=self.sib_recv.at[n],
                    device_id=self.at.sibling(),
                    device_id_type=pl.DeviceIdType.MESH,
                ).wait_recv()

    def drain(self):
        for copy in self.copies:
            copy.wait_send()


def spread_kernel(
    tok, grad, length, dy_out, x_out, lens_out, sbuf, rbuf, a_send, a_recv, g_send, g_recv, s_send, s_recv
):
    at = Place()
    dl = tok.shape[1] // 8
    own_len = jnp.full((16, 128), length[0], jnp.int32).astype(F32).astype(BF)
    for c in range(8):
        cols = slice(c * dl, (c + 1) * dl)
        both = jnp.concatenate([tok[:, cols].astype(F32), grad[:, cols].astype(F32)], axis=0)
        sbuf[c, :, :dl] = both.astype(BF)
        sbuf[c, :, dl:] = own_len
    at.barrier()
    copies = []
    for k in (4, 3, 5, 2, 6, 1, 7):
        peer = lax.rem(at.dp + k, 8)
        copies.append(
            send(sbuf.at[peer], rbuf.at[at.dp], a_send.at[k], a_recv.at[k], {"dp": peer})
        )
    rbuf[at.dp] = sbuf[at.dp]
    for k in (4, 3, 5, 2, 6, 1, 7):
        source = lax.rem(at.dp + 8 - k, 8)
        pltpu.make_async_remote_copy(
            src_ref=rbuf.at[source],
            dst_ref=rbuf.at[source],
            send_sem=a_send.at[k],
            recv_sem=a_recv.at[k],
            device_id={"dp": source},
            device_id_type=pl.DeviceIdType.MESH,
        ).wait_recv()
    own = pl.multiple_of((at.core * 8 + at.chip) * 64, 64)
    gather = Gather(at, dy_out, 64, (g_send, g_recv), (s_send, s_recv))
    blocks = [rbuf[r].astype(F32) for r in range(8)]
    for k in range(4):
        a, b = blocks[2 * k], blocks[2 * k + 1]
        rows = pl.ds(pl.multiple_of(own + 16 * k, 16), 16)
        dy_out[rows, :] = jnp.concatenate([a[8:, :dl], b[8:, :dl]], axis=0).astype(BF)
    gather.stage(0)
    for k in range(4):
        a, b = blocks[2 * k], blocks[2 * k + 1]
        x_out[16 * k : 16 * k + 16, :] = jnp.concatenate([a[:8, :dl], b[:8, :dl]], axis=0).astype(BF)
    for r in range(8):
        lens_out[r : r + 1, :] = blocks[r][0:1, dl:].astype(jnp.int32)
    for n in range(1, 5):
        gather.stage(n)
    gather.drain()
    for copy in copies:
        copy.wait_send()


def spread(tokens, out_grad, lengths):
    dl = tokens.shape[1] // 8
    dma = pltpu.SemaphoreType.DMA
    vmem = pl.BlockSpec(memory_space=pltpu.VMEM)
    return pl.pallas_call(
        spread_kernel,
        out_shape=(
            jax.ShapeDtypeStruct((1024, dl), BF),
            jax.ShapeDtypeStruct((64, dl), BF),
            jax.ShapeDtypeStruct((8, 128), jnp.int32),
        ),
        in_specs=[vmem, vmem, pl.BlockSpec(memory_space=pltpu.SMEM)],
        out_specs=(vmem, vmem, vmem),
        scratch_shapes=[
            pltpu.VMEM((8, 16, dl + 128), BF),
            pltpu.VMEM((8, 16, dl + 128), BF),
            dma((8,)),
            dma((8,)),
            dma((7,)),
            dma((7,)),
            dma((8,)),
            dma((8,)),
        ],
        compiler_params=pltpu.CompilerParams(
            collective_id=0, has_side_effects=True, vmem_limit_bytes=24 * MIB
        ),
    )(tokens, out_grad, lengths)


def rank_of(index, lens, slabs):
    if slabs:
        slab = index >> 6
        response = (index >> 3) & 7
        place = ((slab & 7) * 2 + (slab >> 3)) * 8 + (index & 7)
    else:
        response = index >> 7
        place = index & 127
    rank = jnp.full(index.shape, -1, jnp.int32)
    first = 0
    for r in range(8):
        live = (response == r) & (place < lens[r])
        rank = jnp.where(live, place + first, rank)
        first = first + lens[r]
    return rank


def main_kernel(
    lens,
    dy,
    xs,
    gp,
    up,
    wg_hbm,
    wu_hbm,
    wd_hbm,
    gt_out,
    dg_out,
    du_out,
    hid_out,
    xc_out,
    dyc_out,
    x,
    p_slab,
    p_own,
    p_back,
    dyc,
    xc,
    wg,
    wu,
    wd,
    raw,
    gate,
    upc,
    hid,
    term,
    rs_out,
    rs_in,
    dh,
    part_b,
    half_out,
    half_in,
    total,
    mp_out,
    mp_in,
    fin_out,
    fin_in,
    w_sem,
    raw_sem,
    out_sem,
    rs_send,
    rs_recv,
    ag_send,
    ag_recv,
    g_send,
    g_recv,
    s_send,
    s_recv,
    h_send,
    h_recv,
    m_send,
    m_recv,
    f_send,
    f_recv,
):
    at = Place()
    cap = dyc.shape[0]
    rows = cap // 8
    fw = term.shape[2]
    dl = dyc.shape[1]
    dw = dl // ND
    tile = min(256, fw)
    sent = []

    weights = [
        pltpu.make_async_copy(src, dst, w_sem.at[n])
        for n, (src, dst) in enumerate(((wd_hbm, wd), (wg_hbm, wg), (wu_hbm, wu)))
    ]
    weights[0].start()

    def raw_copy(n):
        j, which = n // 2, n % 2
        src = (gp, up)[which].at[:, j * fw : (j + 1) * fw]
        return pltpu.make_async_copy(src, raw.at[n % 4], raw_sem.at[n])

    for n in range(4):
        raw_copy(n).start()
    weights[1].start()
    weights[2].start()

    blk = 128
    rank_slab = rank_of(lax.broadcasted_iota(jnp.int32, (1, 1024), 1), lens, True)

    @pl.loop(0, cap // blk)
    def _(i):
        start = pl.multiple_of(i * blk, blk)
        index = lax.broadcasted_iota(jnp.int32, (blk, 1024), 0) + start
        p_slab[pl.ds(start, blk), :] = jnp.where(index == rank_slab, 1.0, 0.0).astype(BF)

    at.barrier()
    own = pl.multiple_of((at.core * 8 + at.chip) * 64, 64)
    x[pl.ds(own, 64), :] = xs[...]
    gather = Gather(at, x, 64, (g_send, g_recv), (s_send, s_recv))

    @pl.loop(0, dl // tile)
    def _(i):
        cols = pl.ds(pl.multiple_of(i * tile, tile), tile)
        dyc[:, cols] = dot(p_slab[...], dy[:, cols]).astype(BF)

    outs = [pltpu.make_async_copy(dyc, dyc_out, out_sem.at[0])]
    outs[0].start()
    weights[0].wait()

    def chunk(j, offset):
        owner = at.dp_at(-offset[0], offset[1])
        return term[j, pl.ds(pl.multiple_of(owner * rows, rows), rows), :]

    def rs_hop(j, e, value):
        rs_out[j, e] = value.astype(BF)
        src, dst = DP_TREE[e]
        sent.append(
            send(rs_out.at[j, e], rs_in.at[j, e], rs_send.at[j, e], rs_recv.at[j, e], at.dp_hop(src, dst))
        )

    def rs_arrive(j, e):
        pltpu.make_async_remote_copy(
            src_ref=rs_out.at[j, e],
            dst_ref=rs_in.at[j, e],
            send_sem=rs_send.at[j, e],
            recv_sem=rs_recv.at[j, e],
            device_id=at.sibling(),
            device_id_type=pl.DeviceIdType.MESH,
        ).wait_recv()
        return rs_in[j, e].astype(F32)

    for j in range(NF):

        @pl.loop(0, fw // tile)
        def _(i):
            cols = pl.ds(pl.multiple_of(i * tile, tile), tile)
            units = pl.ds(pl.multiple_of(j * fw + i * tile, tile), tile)
            term[j, :, cols] = dot_nt(dyc[...], wd[units, :])

        for e in range(4):
            rs_hop(j, e, chunk(j, DP_TREE[e][0]))

    gather.stage(0)

    rank_own = rank_of(lax.broadcasted_iota(jnp.int32, (1, 1024), 1), lens, False)

    @pl.loop(0, cap // blk)
    def _(i):
        start = pl.multiple_of(i * blk, blk)
        index = lax.broadcasted_iota(jnp.int32, (blk, 1024), 0) + start
        p_own[pl.ds(start, blk), :] = jnp.where(index == rank_own, 1.0, 0.0).astype(BF)

    def pack(j):
        for which, dst in ((0, gate), (1, upc)):
            n = 2 * j + which
            raw_copy(n).wait()

            @pl.loop(0, fw // tile)
            def _(i):
                cols = pl.ds(pl.multiple_of(i * tile, tile), tile)
                dst[j, :, cols] = dot(p_own[...], raw[n % 4, :, cols]).astype(BF)

            if n + 4 < 2 * NF:
                raw_copy(n + 4).start()

    def hidden(j):
        @pl.loop(0, cap // 64)
        def _(i):
            here = pl.ds(pl.multiple_of(i * 64, 64), 64)
            g = gate[j, here, :].astype(F32)
            u = upc[j, here, :].astype(F32)
            hid[j, here, :] = (g * jax.nn.sigmoid(g) * u).astype(BF)

        copy = pltpu.make_async_copy(
            hid.at[j], hid_out.at[:, j * fw : (j + 1) * fw], out_sem.at[2 + j]
        )
        copy.start()
        outs.append(copy)

    for j in range(NF):
        rs_hop(j, 4, chunk(j, (2, 0)) + rs_arrive(j, 0))
    pack(0)
    gather.stage(1)
    for j in range(NF):
        rs_hop(j, 5, chunk(j, (0, 1)) + rs_arrive(j, 1) + rs_arrive(j, 2))
    for j in range(NF):
        rs_hop(j, 6, chunk(j, (1, 0)) + rs_arrive(j, 4))
    pack(1)
    gather.stage(2)

    def dh_rows(j, offset):
        owner = at.dp_at(-offset[0], offset[1])
        return dh.at[j, pl.ds(pl.multiple_of(owner * rows, rows), rows), :]

    def ag_hop(j, e):
        dst, src = DP_TREE[e]
        ref = dh_rows(j, src)
        sent.append(send(ref, ref, ag_send.at[j, e], ag_recv.at[j, e], at.dp_hop(src, dst)))

    def ag_arrive(j, e):
        ref = dh_rows(j, DP_TREE[e][0])
        pltpu.make_async_remote_copy(
            src_ref=ref,
            dst_ref=ref,
            send_sem=ag_send.at[j, e],
            recv_sem=ag_recv.at[j, e],
            device_id=at.sibling(),
            device_id_type=pl.DeviceIdType.MESH,
        ).wait_recv()

    for j in range(NF):
        value = chunk(j, (0, 0)) + rs_arrive(j, 3) + rs_arrive(j, 5) + rs_arrive(j, 6)
        dh[j, pl.ds(pl.multiple_of(at.dp * rows, rows), rows), :] = value.astype(BF)
        for e in (6, 5, 3):
            ag_hop(j, e)
    for j in range(2, NF):
        pack(j)
    for j in range(NF):
        hidden(j)
    gather.stage(3)
    for j in range(NF):
        ag_arrive(j, 6)
        ag_hop(j, 4)
        ag_arrive(j, 5)
        ag_hop(j, 1)
        ag_hop(j, 2)
    gather.stage(4)

    @pl.loop(0, dl // tile)
    def _(i):
        cols = pl.ds(pl.multiple_of(i * tile, tile), tile)
        xc[:, cols] = dot(p_slab[...], x[:, cols]).astype(BF)

    copy = pltpu.make_async_copy(xc, xc_out, out_sem.at[1])
    copy.start()
    outs.append(copy)

    back_rows = lax.broadcasted_iota(jnp.int32, (blk, 1), 0)

    @pl.loop(0, 1024 // blk)
    def _(i):
        start = pl.multiple_of(i * blk, blk)
        rank = rank_of(back_rows + start, lens, True)
        index = lax.broadcasted_iota(jnp.int32, (blk, cap), 1)
        p_back[pl.ds(start, blk), :] = jnp.where(index == rank, 1.0, 0.0).astype(BF)

    for j in range(NF):
        ag_arrive(j, 4)
        ag_hop(j, 0)

    weights[1].wait()
    weights[2].wait()
    half = 512

    def half_copy(d):
        return pltpu.make_async_remote_copy(
            src_ref=half_out.at[d],
            dst_ref=half_in.at[d],
            send_sem=h_send.at[d],
            recv_sem=h_recv.at[d],
            device_id=at.sibling(),
            device_id_type=pl.DeviceIdType.MESH,
        )

    for j in range(NF):
        for e in (3, 1, 2, 0):
            ag_arrive(j, e)

        @pl.loop(0, cap // 64)
        def _(i):
            here = pl.ds(pl.multiple_of(i * 64, 64), 64)
            g = gate[j, here, :].astype(F32)
            u = upc[j, here, :].astype(F32)
            d = dh[j, here, :].astype(F32)
            sig = jax.nn.sigmoid(g)
            gate[j, here, :] = (d * u * sig * (1.0 + g * (1.0 - sig))).astype(BF)
            upc[j, here, :] = (d * g * sig).astype(BF)

        for n, (src, dst) in enumerate(((gate, dg_out), (upc, du_out))):
            copy = pltpu.make_async_copy(
                src.at[j], dst.at[:, j * fw : (j + 1) * fw], out_sem.at[2 + NF + 2 * j + n]
            )
            copy.start()
            outs.append(copy)

        for d in range(ND):

            @pl.loop(0, dw // tile)
            def _(i):
                cols = pl.ds(pl.multiple_of(i * tile, tile), tile)
                units = pl.ds(pl.multiple_of(d * dw + i * tile, tile), tile)
                cut = slice(j * fw, (j + 1) * fw)
                value = dot_nt(gate[j], wg[units, cut]) + dot_nt(upc[j], wu[units, cut])
                if j:
                    value = value + term[d, :, cols]
                if j < NF - 1:
                    term[d, :, cols] = value
                else:
                    part_b[d, :, cols] = value.astype(BF)

            if j == NF - 1:
                other = pl.ds(pl.multiple_of((1 - at.core) * half, half), half)

                @pl.loop(0, dw // tile)
                def _(i):
                    cols = pl.ds(pl.multiple_of(i * tile, tile), tile)
                    half_out[d, :, cols] = dot(p_back[other, :], part_b[d, :, cols]).astype(BF)

                half_copy(d).start()

    mine = pl.ds(pl.multiple_of(at.core * half, half), half)

    def mp_chunk(d, offset):
        owner = at.chip_at(-offset[0], offset[1])
        return total[d, pl.ds(pl.multiple_of(owner * 64, 64), 64), :]

    def mp_hop(d, e, value):
        mp_out[d, e] = value.astype(BF)
        src, dst = MP_TREE[e]
        sent.append(
            send(mp_out.at[d, e], mp_in.at[d, e], m_send.at[d, e], m_recv.at[d, e], at.mp_hop(src, dst))
        )

    def mp_arrive(d, e):
        pltpu.make_async_remote_copy(
            src_ref=mp_out.at[d, e],
            dst_ref=mp_in.at[d, e],
            send_sem=m_send.at[d, e],
            recv_sem=m_recv.at[d, e],
            device_id=at.sibling(),
            device_id_type=pl.DeviceIdType.MESH,
        ).wait_recv()
        return mp_in[d, e].astype(F32)

    for d in range(ND):

        @pl.loop(0, dw // tile)
        def _(i):
            cols = pl.ds(pl.multiple_of(i * tile, tile), tile)
            total[d, :, cols] = dot(p_back[mine, :], part_b[d, :, cols])

        half_copy(d).wait_recv()

        @pl.loop(0, 8)
        def _(i):
            here = pl.ds(pl.multiple_of(i * 64, 64), 64)
            total[d, here, :] = total[d, here, :] + half_in[d, here, :].astype(F32)

        for e in range(4):
            mp_hop(d, e, mp_chunk(d, MP_TREE[e][0]))
    for d in range(ND):
        mp_hop(d, 4, mp_chunk(d, (1, 1)) + mp_arrive(d, 0))
        mp_hop(d, 5, mp_chunk(d, (1, 0)) + mp_arrive(d, 2))
    for d in range(ND):
        mp_hop(d, 6, mp_chunk(d, (0, 1)) + mp_arrive(d, 1) + mp_arrive(d, 4))
    sums = []
    for d in range(ND):
        sums.append(mp_chunk(d, (0, 0)) + mp_arrive(d, 3) + mp_arrive(d, 5) + mp_arrive(d, 6))

    for r in range(8):
        both = jnp.concatenate([s[r * 8 : r * 8 + 8, :] for s in sums], axis=0)
        fin_out[r] = both.astype(BF)
    for k in (4, 3, 5, 2, 6, 1, 7):
        peer = lax.rem(at.dp + k, 8)
        sent.append(
            send(fin_out.at[peer], fin_in.at[at.dp], f_send.at[k], f_recv.at[k], {"dp": peer})
        )
    fin_in[at.dp] = fin_out[at.dp]
    for k in (4, 3, 5, 2, 6, 1, 7):
        source = lax.rem(at.dp + 8 - k, 8)
        pltpu.make_async_remote_copy(
            src_ref=fin_in.at[source],
            dst_ref=fin_in.at[source],
            send_sem=f_send.at[k],
            recv_sem=f_recv.at[k],
            device_id={"dp": source},
            device_id_type=pl.DeviceIdType.MESH,
        ).wait_recv()
    for c in range(8):
        both = fin_in[c].astype(F32)
        for d in range(ND):
            gt_out[:, c * dl + d * dw : c * dl + (d + 1) * dw] = both[d * 8 : d * 8 + 8, :].astype(BF)

    gather.drain()
    for copy in sent:
        copy.wait_send()
    for d in range(ND):
        half_copy(d).wait_send()
    for copy in outs:
        copy.wait()


def main_call(cap, number, lens, dy, xs, gate_pre, up_pre, wg, wu, wd):
    dl, fl = dy.shape[1], gate_pre.shape[1]
    fw, dw, rows = fl // NF, dl // ND, cap // 8
    dma = pltpu.SemaphoreType.DMA
    vmem, anywhere = pl.BlockSpec(memory_space=pltpu.VMEM), pl.BlockSpec(memory_space=pl.ANY)
    f32, bf = jnp.float32, BF
    buffers = [
        ((1024, dl), bf),
        ((cap, 1024), bf),
        ((cap, 1024), bf),
        ((1024, cap), bf),
        ((cap, dl), bf),
        ((cap, dl), bf),
        ((dl, fl), bf),
        ((dl, fl), bf),
        ((fl, dl), bf),
        ((4, 1024, fw), bf),
        ((NF, cap, fw), bf),
        ((NF, cap, fw), bf),
        ((NF, cap, fw), bf),
        ((NF, cap, max(fw, dw)), f32),
        ((NF, 7, rows, fw), bf),
        ((NF, 7, rows, fw), bf),
        ((NF, cap, fw), bf),
        ((ND, cap, dw), bf),
        ((ND, 512, dw), bf),
        ((ND, 512, dw), bf),
        ((ND, 512, dw), f32),
        ((ND, 7, 64, dw), bf),
        ((ND, 7, 64, dw), bf),
        ((8, 16, dw), bf),
        ((8, 16, dw), bf),
    ]
    sems = [
        (3,),
        (2 * NF,),
        (2 + 3 * NF,),
        (NF, 7),
        (NF, 7),
        (NF, 7),
        (NF, 7),
        (7,),
        (7,),
        (8,),
        (8,),
        (ND,),
        (ND,),
        (ND, 7),
        (ND, 7),
        (8,),
        (8,),
    ]
    return pl.pallas_call(
        main_kernel,
        out_shape=(
            jax.ShapeDtypeStruct((8, dl * 8), bf),
            jax.ShapeDtypeStruct((cap, fl), bf),
            jax.ShapeDtypeStruct((cap, fl), bf),
            jax.ShapeDtypeStruct((cap, fl), bf),
            jax.ShapeDtypeStruct((cap, dl), bf),
            jax.ShapeDtypeStruct((cap, dl), bf),
        ),
        in_specs=[pl.BlockSpec(memory_space=pltpu.SMEM), vmem, vmem] + [anywhere] * 5,
        out_specs=(vmem,) + (anywhere,) * 5,
        scratch_shapes=[pltpu.VMEM(s, t) for s, t in buffers] + [dma(s) for s in sems],
        compiler_params=pltpu.CompilerParams(
            collective_id=1 + number, has_side_effects=True, vmem_limit_bytes=62 * MIB
        ),
    )(lens, dy, xs, gate_pre, up_pre, wg, wu, wd)


def branch(cap, number, lens, dy, xs, gate_pre, up_pre, wg, wu, wd):
    grad_tokens, dgate, dup, hidden, x, masked = main_call(
        cap, number, lens, dy, xs, gate_pre, up_pre, wg, wu, wd
    )
    grad_gate = jnp.einsum("td,tf->df", x, dgate, preferred_element_type=F32).astype(BF)
    grad_up = jnp.einsum("td,tf->df", x, dup, preferred_element_type=F32).astype(BF)
    grad_down = jnp.einsum("tf,td->fd", hidden, masked, preferred_element_type=F32).astype(BF)
    return grad_tokens, grad_gate, grad_up, grad_down


def local(tokens, out_grad, gate_pre, up_pre, gate_weight, up_weight, down_weight, lengths):
    dy, xs, lens = spread(tokens, out_grad, lengths)
    lens = lens[:, 0]
    need = jnp.sum(lens)
    which = jnp.sum((need > jnp.array(SIZES[:-1], jnp.int32)).astype(jnp.int32))
    return lax.switch(
        which,
        [functools.partial(branch, cap, n) for n, cap in enumerate(SIZES)],
        lens,
        dy,
        xs,
        gate_pre,
        up_pre,
        gate_weight,
        up_weight,
        down_weight,
    )


def solution(mesh):
    in_specs = (
        P(("dp", "mp"), None),
        P(("dp", "mp"), None),
        P(None, "mp"),
        P(None, "mp"),
        P("dp", "mp"),
        P("dp", "mp"),
        P("mp", "dp"),
        P("dp"),
    )
    out_specs = (P(("dp", "mp"), None), P("dp", "mp"), P("dp", "mp"), P("mp", "dp"))
    return jax.shard_map(local, mesh=mesh, in_specs=in_specs, out_specs=out_specs, check_vma=False)
```

```python
import functools

import jax
import jax.numpy as jnp
from jax import lax
from jax.experimental import pallas as pl
from jax.experimental.pallas import tpu as pltpu
from jax.sharding import PartitionSpec as P

SEQ_LEN = 128
NZ, NY = 4, 2
NF = 2
ND = 2
SIZE = 640
BF, F32 = jnp.bfloat16, jnp.float32
MIB = 1 << 20

TREE = (
    ((2, 1), (2, 0)),
    ((1, 1), (0, 1)),
    ((3, 1), (0, 1)),
    ((3, 0), (0, 0)),
    ((2, 0), (1, 0)),
    ((0, 1), (0, 0)),
    ((1, 0), (0, 0)),
)
FLAT = TREE[:4] + (((2, 0), (0, 0)),) + TREE[5:]


class Place:
    def __init__(self):
        self.dp = lax.axis_index("dp")
        self.mp = lax.axis_index("mp")
        self.z, self.yl = self.dp // NY, self.dp % NY
        self.core = self.mp % 2
        self.chip = self.mp // 2
        self.yh, self.x = self.chip // 4, self.chip % 4
        self.sign = 1 - 2 * self.core

    def dp_at(self, da, db):
        z = lax.rem(self.z + self.sign * da + 4, 4)
        return z * NY + (1 - self.yl if db else self.yl)

    def chip_at(self, da, db):
        x = lax.rem(self.x + self.sign * da + 4, 4)
        return (1 - self.yh if db else self.yh) * 4 + x

    def dp_hop(self, src, dst):
        return {"dp": self.dp_at(dst[0] - src[0], src[1] ^ dst[1])}

    def mp_hop(self, src, dst):
        return {"mp": self.chip_at(dst[0] - src[0], src[1] ^ dst[1]) * 2 + self.core}

    def sibling(self):
        return {"mp": self.chip * 2 + 1 - self.core}

    def greet(self):
        sem = pltpu.get_barrier_semaphore()
        peers = [{"dp": lax.rem(self.dp + k, 8)} for k in range(1, 8)]
        near = ((1, 0), (2, 0), (3, 0), (0, 1))
        peers += [self.sibling()]
        peers += [{"mp": self.chip_at(a, b) * 2 + self.core} for a, b in near]
        for peer in peers:
            pl.semaphore_signal(sem, inc=1, device_id=peer, device_id_type=pl.DeviceIdType.MESH)
        self.peers = len(peers)

    def meet(self):
        pl.semaphore_wait(pltpu.get_barrier_semaphore(), self.peers)


def remote(src, dst, send_sem, recv_sem, device):
    return pltpu.make_async_remote_copy(
        src_ref=src,
        dst_ref=dst,
        send_sem=send_sem,
        recv_sem=recv_sem,
        device_id=device,
        device_id_type=pl.DeviceIdType.MESH,
    )


def send(*args):
    copy = remote(*args)
    copy.start()
    return copy


def dot_nt(a, b):
    return lax.dot_general(a, b, (((1,), (1,)), ((), ())), preferred_element_type=F32)


def dot(a, b):
    return jnp.dot(a, b, preferred_element_type=F32)


class Gather:
    def __init__(self, at, buf, rows, sems):
        self.at, self.buf, self.rows = at, buf, rows
        self.send_sem, self.recv_sem, self.sib_send, self.sib_recv = sems
        self.copies = []

    def slab(self, chip, core):
        start = pl.multiple_of((core * 8 + chip) * self.rows, self.rows)
        return self.buf.at[pl.ds(start, self.rows), :]

    def slab_from(self, offset):
        return self.slab(self.at.chip_at(-offset[0], offset[1]), self.at.core)

    def put(self, value):
        start = pl.multiple_of((self.at.core * 8 + self.at.chip) * self.rows, self.rows)
        self.buf[pl.ds(start, self.rows), :] = value

    def hop(self, e):
        dst, src = FLAT[e]
        ref = self.slab_from(src)
        self.copies.append(
            send(ref, ref, self.send_sem.at[e], self.recv_sem.at[e], self.at.mp_hop(src, dst))
        )

    def to_sibling(self, n, offset):
        ref = self.slab_from(offset)
        self.copies.append(
            send(ref, ref, self.sib_send.at[n], self.sib_recv.at[n], self.at.sibling())
        )

    def arrive(self, e):
        offset = FLAT[e][0]
        arrival(self.slab_from(offset), self.send_sem.at[e], self.recv_sem.at[e], self.at)
        self.to_sibling(e, offset)

    def stage(self, n):
        if n == 0:
            for e in (5, 4, 6, 3):
                self.hop(e)
            self.to_sibling(7, (0, 0))
        elif n == 1:
            self.arrive(5)
            self.hop(1)
            self.hop(2)
            self.arrive(6)
            self.arrive(3)
        elif n == 2:
            self.arrive(4)
            self.hop(0)
        elif n == 3:
            for e in (1, 2, 0):
                self.arrive(e)
        else:
            for n, offset in enumerate([src for src, _ in FLAT] + [(0, 0)]):
                ref = self.slab(self.at.chip_at(*offset), 1 - self.at.core)
                arrival(ref, self.sib_send.at[n], self.sib_recv.at[n], self.at)

    def drain(self):
        for copy in self.copies:
            copy.wait_send()


def arrival(ref, send_sem, recv_sem, at):
    remote(ref, ref, send_sem, recv_sem, at.sibling()).wait_recv()


def live_rows(length, parity):
    rest = length & 15
    extra = jnp.where(parity == 0, jnp.minimum(rest, 8), jnp.maximum(rest - 8, 0))
    return (length >> 4) * 8 + extra


def rank_of(index, lens, h, slabs):
    if slabs:
        slab = index >> 5
        core = slab >> 3
        response = ((index >> 3) & 3) * 2 + ((core + h) & 1)
        place = ((slab & 7) * 2 + core) * 8 + (index & 7)
    else:
        response = index >> 7
        place = index & 127
    rank = jnp.full(index.shape, -1, jnp.int32)
    first = 0
    for r in range(8):
        parity = (r + h) & 1
        live = (response == r) & (place < lens[r]) & (((place >> 3) & 1) == parity)
        rank = jnp.where(live, (place >> 4) * 8 + (place & 7) + first, rank)
        first = first + live_rows(lens[r], parity)
    return rank


def fold(value):
    mid = value.shape[1] // 2
    return jnp.concatenate([value[:, :mid], value[:, mid:]], axis=0)


def main_kernel(
    tok_hbm,
    grad_hbm,
    length,
    gp,
    up,
    wg_hbm,
    wu_hbm,
    wd_hbm,
    gt_out,
    gg_out,
    gu_out,
    gd_out,
    over_out,
    tok,
    grad,
    sbuf,
    rbuf,
    dyb,
    xb,
    p_slab,
    p_own,
    p_back,
    dyc,
    wg,
    wu,
    wd,
    raw,
    act,
    hid,
    dact,
    term,
    rs_out,
    rs_in,
    dh,
    half_out,
    half_in,
    mp_out,
    mp_in,
    fin_out,
    fin_in,
    in_sem,
    a_send,
    a_recv,
    w_sem,
    raw_sem,
    out_sem,
    rs_send,
    rs_recv,
    ag_send,
    ag_recv,
    dy_send,
    dy_recv,
    dys_send,
    dys_recv,
    x_send,
    x_recv,
    xs_send,
    xs_recv,
    h_send,
    h_recv,
    m_send,
    m_recv,
    f_send,
    f_recv,
):
    at = Place()
    cap = dyc.shape[0] // 2
    rows = cap // 8
    fw = term.shape[3]
    dl = dyc.shape[1]
    dw = dl // ND
    sent = []

    loads = [
        pltpu.make_async_copy(src, dst, in_sem.at[n])
        for n, (src, dst) in enumerate(((tok_hbm, tok), (grad_hbm, grad)))
    ]
    for copy in loads:
        copy.start()
    at.greet()
    for copy in loads:
        copy.wait()
    own_len = jnp.full((16, 128), length[0], jnp.int32).astype(F32).astype(BF)
    for c in range(8):
        cols = slice(c * dl, (c + 1) * dl)
        both = jnp.concatenate([tok[:, cols].astype(F32), grad[:, cols].astype(F32)], axis=0)
        sbuf[c, :, :dl] = both.astype(BF)
        sbuf[c, :, dl:] = own_len
    at.meet()
    for k in (4, 3, 5, 2, 6, 1, 7):
        peer = lax.rem(at.dp + k, 8)
        sent.append(
            send(sbuf.at[peer], rbuf.at[at.dp], a_send.at[k], a_recv.at[k], {"dp": peer})
        )
    rbuf[at.dp] = sbuf[at.dp]

    def piece(j):
        return pl.ds(pl.multiple_of(j * fw, fw), fw)

    weights = [pltpu.make_async_copy(wd_hbm, wd, w_sem.at[0])]
    for j in range(NF):
        for n, (src, dst) in enumerate(((wg_hbm, wg), (wu_hbm, wu))):
            sem = w_sem.at[1 + 2 * j + n]
            weights.append(pltpu.make_async_copy(src.at[:, piece(j)], dst.at[j], sem))
    raws = [
        pltpu.make_async_copy(
            (gp, up)[n % 2].at[:, (n // 2) * fw : (n // 2 + 1) * fw], raw.at[n], raw_sem.at[n]
        )
        for n in range(2 * NF)
    ]
    weights[0].start()
    for copy in raws:
        copy.start()
    for k in (4, 3, 5, 2, 6, 1, 7):
        source = lax.rem(at.dp + 8 - k, 8)
        arrival(rbuf.at[source], a_send.at[k], a_recv.at[k], at)

    def slab_of(h, first):
        parity = (at.core + h) & 1
        blocks = [rbuf[2 * k + parity].astype(F32)[first : first + 8, :dl] for k in range(4)]
        return jnp.concatenate(blocks, axis=0).astype(BF)


    def one_hot(ref, slot, h, slabs):
        size = ref.shape[2]
        rank = rank_of(lax.broadcasted_iota(jnp.int32, (1, size), 1), lens, h, slabs)
        blk = 64

        @pl.loop(0, cap // blk)
        def _(i):
            start = pl.multiple_of(i * blk, blk)
            index = lax.broadcasted_iota(jnp.int32, (blk, size), 0) + start
            ref[slot, pl.ds(start, blk), :] = jnp.where(index == rank, 1.0, 0.0).astype(BF)

    def back_matrix(h):
        blk = 128

        @pl.loop(0, 512 // blk)
        def _(i):
            start = pl.multiple_of(i * blk, blk)
            index = lax.broadcasted_iota(jnp.int32, (blk, 1), 0) + start
            rank = rank_of(index, lens, h, True)
            lane = lax.broadcasted_iota(jnp.int32, (blk, cap), 1)
            p_back[pl.ds(start, blk), :] = jnp.where(lane == rank, 1.0, 0.0).astype(BF)

    gather_dy, gather_x = [], []
    for h in range(2):
        sems = [sem.at[h] for sem in (dy_send, dy_recv, dys_send, dys_recv)]
        gather_dy.append(Gather(at, dyb.at[h], 32, sems))
        gather_dy[h].put(slab_of(h, 8))
        gather_dy[h].stage(0)
    for h in range(2):
        sems = [sem.at[h] for sem in (x_send, x_recv, xs_send, xs_recv)]
        gather_x.append(Gather(at, xb.at[h], 32, sems))
        gather_x[h].put(slab_of(h, 0))
    lens = [jnp.max(rbuf[r].astype(F32)[0:1, dl:]).astype(jnp.int32) for r in range(8)]
    need = [sum(live_rows(lens[r], (r + h) & 1) for r in range(8)) for h in range(2)]
    over_out[0] = (jnp.maximum(need[0], need[1]) > cap).astype(jnp.int32)

    def half_rows(h):
        return slice(h * cap, (h + 1) * cap)

    def chunk(h, j, offset):
        owner = at.dp_at(-offset[0], offset[1])
        return fold(term[h, j, pl.ds(pl.multiple_of(owner * rows, rows), rows), :])

    def rs_copy(h, j, e):
        src, dst = TREE[e]
        return remote(
            rs_out.at[h, j, e],
            rs_in.at[h, j, e],
            rs_send.at[h, j, e],
            rs_recv.at[h, j, e],
            at.dp_hop(src, dst),
        )

    def rs_hop(h, j, e, value):
        rs_out[h, j, e] = value.astype(BF)
        rs_copy(h, j, e).start()

    def rs_arrive(h, j, e):
        arrival(rs_in.at[h, j, e], rs_send.at[h, j, e], rs_recv.at[h, j, e], at)
        return rs_in[h, j, e].astype(F32)

    def terms(h):
        dyc[half_rows(h), :] = dot(p_slab[h], dyb[h]).astype(BF)
        if h == 0:
            weights[0].wait()

        @pl.loop(0, NF)
        def _(j):
            term[h, j] = dot_nt(dyc[half_rows(h), :], wd[piece(j), :])
            for e in range(4):
                rs_hop(h, j, e, chunk(h, j, TREE[e][0]))

    def rs4(h):
        @pl.loop(0, NF)
        def _(j):
            rs_hop(h, j, 4, chunk(h, j, (2, 0)) + rs_arrive(h, j, 0))

    def rs5(h):
        @pl.loop(0, NF)
        def _(j):
            rs_hop(h, j, 5, chunk(h, j, (0, 1)) + rs_arrive(h, j, 1) + rs_arrive(h, j, 2))

    def rs6(h):
        @pl.loop(0, NF)
        def _(j):
            rs_hop(h, j, 6, chunk(h, j, (1, 0)) + rs_arrive(h, j, 4))

    def ag_ref(h, j, offset):
        return dh.at[h, j, at.dp_at(-offset[0], offset[1])]

    def ag_copy(h, j, e):
        dst, src = TREE[e]
        ref = ag_ref(h, j, src)
        return remote(ref, ref, ag_send.at[h, j, e], ag_recv.at[h, j, e], at.dp_hop(src, dst))

    def ag_hop(h, j, e):
        ag_copy(h, j, e).start()

    def ag_arrive(h, j, e):
        arrival(ag_ref(h, j, TREE[e][0]), ag_send.at[h, j, e], ag_recv.at[h, j, e], at)

    def rs_own(h):
        @pl.loop(0, NF)
        def _(j):
            value = chunk(h, j, (0, 0)) + rs_arrive(h, j, 3)
            value = value + rs_arrive(h, j, 5) + rs_arrive(h, j, 6)
            dh[h, j, at.dp] = value.astype(BF)
            for e in (6, 5, 3):
                ag_hop(h, j, e)

    def ag_forward(h):
        @pl.loop(0, NF)
        def _(j):
            ag_arrive(h, j, 6)
            ag_hop(h, j, 4)
            ag_arrive(h, j, 5)
            ag_hop(h, j, 1)
            ag_hop(h, j, 2)

    def ag_forward_last(h):
        @pl.loop(0, NF)
        def _(j):
            ag_arrive(h, j, 4)
            ag_hop(h, j, 0)

    def pack(h, first, last):
        if h == 0 and first == 0:
            for copy in raws:
                copy.wait()

        @pl.loop(first, last)
        def _(n):
            value = dot(p_own[0], raw[n])
            for o in range(8):
                act[h, n, o] = fold(value[o * rows : (o + 1) * rows, :]).astype(BF)

    def unfold_store(ref, h, j, k, pair):
        here = pl.ds(pl.multiple_of(h * cap + k * 2 * rows, 16), 2 * rows)
        mid = fw // 2
        for n in range(2):
            part = [v[n * rows : (n + 1) * rows, :] for v in pair]
            ref[j, here, n * mid : (n + 1) * mid] = jnp.concatenate(part, axis=0).astype(BF)

    def hidden(h):
        @pl.loop(0, 4 * NF)
        def _(i):
            j, k = i // 4, i % 4
            pair = []
            for n in range(2):
                g = act[h, 2 * j, 2 * k + n].astype(F32)
                u = act[h, 2 * j + 1, 2 * k + n].astype(F32)
                pair.append(g * jax.nn.sigmoid(g) * u)
            unfold_store(hid, h, j, k, pair)

    def gate_backward(h, j):
        @pl.loop(0, 4)
        def _(k):
            gates, ups = [], []
            for n in range(2):
                g = act[h, 2 * j, 2 * k + n].astype(F32)
                u = act[h, 2 * j + 1, 2 * k + n].astype(F32)
                d = dh[h, j, 2 * k + n].astype(F32)
                sig = jax.nn.sigmoid(g)
                gates.append(d * u * sig * (1.0 + g * (1.0 - sig)))
                ups.append(d * g * sig)
            unfold_store(dact, h, 2 * j, k, gates)
            unfold_store(dact, h, 2 * j + 1, k, ups)

    def half_copy(h, d):
        return remote(
            half_out.at[h, d], half_in.at[h, d], h_send.at[h, d], h_recv.at[h, d], at.sibling()
        )

    def unpack(h, d, core):
        value = term[h, d, :, :dw]
        high = value.astype(BF)
        low = (value - high.astype(F32)).astype(BF)
        back = p_back[pl.ds(pl.multiple_of(core * 256, 256), 256), :]
        return dot(back, high) + dot(back, low)

    def parts(h):
        here = half_rows(h)
        if h == 0:
            for copy in weights[1:]:
                copy.wait()

        @pl.loop(0, NF)
        def _(j):
            for e in (3, 1, 2, 0):
                ag_arrive(h, j, e)
            gate_backward(h, j)

            @pl.loop(0, ND)
            def _(d):
                units = pl.ds(pl.multiple_of(d * dw, dw), dw)
                value = dot_nt(dact[2 * j, here, :], wg[j, units, :])
                value = value + dot_nt(dact[2 * j + 1, here, :], wu[j, units, :])
                term[h, d, :, :dw] = value + jnp.where(j > 0, term[h, d, :, :dw], 0.0)

        @pl.loop(0, ND)
        def _(d):
            half_out[h, d] = unpack(h, d, 1 - at.core).astype(BF)
            half_copy(h, d).start()

    def mp_chunk(h, d, offset):
        owner = at.chip_at(-offset[0], offset[1])
        return term[h, d, pl.ds(pl.multiple_of(owner * 32, 32), 32), :dw]

    def mp_copy(h, d, e):
        src, dst = FLAT[e]
        return remote(
            mp_out.at[h, d, e],
            mp_in.at[h, d, e],
            m_send.at[h, d, e],
            m_recv.at[h, d, e],
            at.mp_hop(src, dst),
        )

    def mp_hop(h, d, e, value):
        mp_out[h, d, e] = value.astype(BF)
        mp_copy(h, d, e).start()

    def mp_arrive(h, d, e):
        arrival(mp_in.at[h, d, e], m_send.at[h, d, e], m_recv.at[h, d, e], at)
        return mp_in[h, d, e].astype(F32)

    def mp_leaves(h):
        @pl.loop(0, ND)
        def _(d):
            term[h, d, :256, :dw] = unpack(h, d, at.core)

        @pl.loop(0, ND)
        def _(d):
            half_copy(h, d).wait_recv()
            term[h, d, :256, :dw] = term[h, d, :256, :dw] + half_in[h, d].astype(F32)
            for e in (0, 1, 2, 6, 3):
                mp_hop(h, d, e, mp_chunk(h, d, FLAT[e][0]))

    def mp4(h):
        @pl.loop(0, ND)
        def _(d):
            mp_hop(h, d, 4, mp_chunk(h, d, (2, 0)) + mp_arrive(h, d, 0))

    def mp5(h):
        @pl.loop(0, ND)
        def _(d):
            mp_hop(h, d, 5, mp_chunk(h, d, (0, 1)) + mp_arrive(h, d, 1) + mp_arrive(h, d, 2))

    def mp_own(h):
        sums = []
        for d in range(ND):
            value = mp_chunk(h, d, (0, 0)) + mp_arrive(h, d, 3) + mp_arrive(h, d, 6)
            sums.append(value + mp_arrive(h, d, 4) + mp_arrive(h, d, 5))
        for k in range(4):
            both = jnp.concatenate([s[k * 8 : k * 8 + 8, :] for s in sums], axis=0)
            fin_out[2 * k + ((at.core + h) & 1)] = both.astype(BF)

    def tn(a, b):
        return lax.dot_general(a, b, (((0,), (0,)), ((), ())), preferred_element_type=F32).astype(BF)

    def out_copies(j):
        return [
            pltpu.make_async_copy(raw.at[2 * j], gg_out.at[:, piece(j)], out_sem.at[3 * j]),
            pltpu.make_async_copy(raw.at[2 * j + 1], gu_out.at[:, piece(j)], out_sem.at[3 * j + 1]),
            pltpu.make_async_copy(wd.at[piece(j), :], gd_out.at[piece(j), :], out_sem.at[3 * j + 2]),
        ]

    def weight_grad(j):
        for n in range(2):
            raw[2 * j + n] = tn(dyc[...], dact[2 * j + n])
            out_copies(j)[n].start()

    def down_grads():
        @pl.loop(0, NF)
        def _(j):
            wd[piece(j), :] = tn(hid[j], dyc[...])
            out_copies(j)[2].start()

    a, b = 0, 1
    one_hot(p_slab, a, a, True)
    one_hot(p_own, 0, a, False)
    gather_dy[a].stage(1)
    gather_dy[b].stage(1)
    for copy in weights[1:]:
        copy.start()
    pack(a, 0, NF)
    gather_dy[a].stage(2)
    gather_dy[b].stage(2)
    pack(a, NF, 2 * NF)
    gather_dy[a].stage(3)
    one_hot(p_slab, b, b, True)
    gather_dy[b].stage(3)
    one_hot(p_own, 0, b, False)
    gather_dy[a].stage(4)
    terms(a)
    gather_dy[b].stage(4)
    terms(b)
    for h in range(2):
        gather_x[h].stage(0)
    rs4(a)
    pack(b, 0, NF)
    rs5(a)
    rs6(a)
    rs4(b)
    for h in range(2):
        gather_x[h].stage(1)
    pack(b, NF, 2 * NF)
    rs5(b)
    rs_own(a)
    rs6(b)
    hidden(a)
    ag_forward(a)
    for h in range(2):
        gather_x[h].stage(2)
    hidden(b)
    rs_own(b)
    ag_forward_last(a)
    back_matrix(a)
    for h in range(2):
        gather_x[h].stage(3)
    ag_forward(b)
    parts(a)
    ag_forward_last(b)
    mp_leaves(a)
    back_matrix(b)
    down_grads()
    for h in range(2):
        gather_x[h].stage(4)
        dyc[half_rows(h), :] = dot(p_slab[h], xb[h]).astype(BF)
    mp4(a)
    parts(b)
    mp5(a)
    mp_leaves(b)
    mp_own(a)
    mp4(b)
    mp5(b)

    @pl.loop(0, NF)
    def _(j):
        weight_grad(j)

    mp_own(b)
    for k in (4, 3, 5, 2, 6, 1, 7):
        peer = lax.rem(at.dp + k, 8)
        sent.append(
            send(fin_out.at[peer], fin_in.at[at.dp], f_send.at[k], f_recv.at[k], {"dp": peer})
        )
    fin_in[at.dp] = fin_out[at.dp]
    for k in (4, 3, 5, 2, 6, 1, 7):
        source = lax.rem(at.dp + 8 - k, 8)
        arrival(fin_in.at[source], f_send.at[k], f_recv.at[k], at)
    for c in range(8):
        both = fin_in[c].astype(F32)
        for d in range(ND):
            gt_out[:, c * dl + d * dw : c * dl + (d + 1) * dw] = both[d * 8 : d * 8 + 8, :].astype(BF)
    for gather in gather_dy + gather_x:
        gather.drain()
    for copy in sent:
        copy.wait_send()

    @pl.loop(0, 2 * NF)
    def _(i):
        h, j = i // NF, i % NF
        for e in range(7):
            rs_copy(h, j, e).wait_send()
            ag_copy(h, j, e).wait_send()

    @pl.loop(0, 2 * ND)
    def _(i):
        h, d = i // ND, i % ND
        half_copy(h, d).wait_send()
        for e in range(7):
            mp_copy(h, d, e).wait_send()

    for j in range(NF):
        for copy in out_copies(j):
            copy.wait()


def main_call(size, number, tokens, out_grad, gate_pre, up_pre, wg, wu, wd, lengths):
    dl, fl = tokens.shape[1] // 8, gate_pre.shape[1]
    fw, dw, cap, rows = fl // NF, dl // ND, size // 2, size // 16
    dma = pltpu.SemaphoreType.DMA
    vmem, smem = pl.BlockSpec(memory_space=pltpu.VMEM), pl.BlockSpec(memory_space=pltpu.SMEM)
    anywhere = pl.BlockSpec(memory_space=pl.ANY)
    buffers = [
        (tokens.shape, BF),
        (tokens.shape, BF),
        ((8, 16, dl + 128), BF),
        ((8, 16, dl + 128), BF),
        ((2, 512, dl), BF),
        ((2, 512, dl), BF),
        ((2, cap, 512), BF),
        ((1, cap, 1024), BF),
        ((512, cap), BF),
        ((size, dl), BF),
        ((NF, dl, fw), BF),
        ((NF, dl, fw), BF),
        ((fl, dl), BF),
        ((2 * NF, 1024, fw), BF),
        ((2, 2 * NF, 8, 2 * rows, fw // 2), BF),
        ((NF, size, fw), BF),
        ((2 * NF, size, fw), BF),
        ((2, NF, cap, fw), F32),
        ((2, NF, 7, 2 * rows, fw // 2), BF),
        ((2, NF, 7, 2 * rows, fw // 2), BF),
        ((2, NF, 8, 2 * rows, fw // 2), BF),
        ((2, ND, 256, dw), BF),
        ((2, ND, 256, dw), BF),
        ((2, ND, 7, 32, dw), BF),
        ((2, ND, 7, 32, dw), BF),
        ((8, 16, dw), BF),
        ((8, 16, dw), BF),
    ]
    sems = [(2,), (8,), (8,), (1 + 2 * NF,), (2 * NF,), (3 * NF,)]
    sems += [(2, NF, 7)] * 4
    sems += [(2, 7), (2, 7), (2, 8), (2, 8)] * 2
    sems += [(2, ND), (2, ND), (2, ND, 7), (2, ND, 7), (8,), (8,)]
    return pl.pallas_call(
        main_kernel,
        out_shape=(
            jax.ShapeDtypeStruct((8, dl * 8), BF),
            jax.ShapeDtypeStruct((dl, fl), BF),
            jax.ShapeDtypeStruct((dl, fl), BF),
            jax.ShapeDtypeStruct((fl, dl), BF),
            jax.ShapeDtypeStruct((1,), jnp.int32),
        ),
        in_specs=[anywhere, anywhere, smem] + [anywhere] * 5,
        out_specs=(vmem,) + (anywhere,) * 3 + (smem,),
        scratch_shapes=[pltpu.VMEM(s, t) for s, t in buffers] + [dma(s) for s in sems],
        compiler_params=pltpu.CompilerParams(
            collective_id=number, has_side_effects=True, vmem_limit_bytes=63 * MIB
        ),
    )(tokens, out_grad, lengths, gate_pre, up_pre, wg, wu, wd)


def copy_kernel(*refs):
    count = len(refs) // 3
    bufs, (in_sem, out_sem) = refs[2 * count : 3 * count], refs[3 * count :]
    pieces = in_sem.shape[1]
    todo = []
    for n in range(count):
        src, dst, buf = refs[n], refs[count + n], bufs[n]
        rows = src.shape[0] // pieces
        for k in range(pieces):
            here = pl.ds(k * rows, rows)
            first = pltpu.make_async_copy(src.at[here, :], buf.at[here, :], in_sem.at[n, k])
            then = pltpu.make_async_copy(buf.at[here, :], dst.at[here, :], out_sem.at[n, k])
            first.start()
            todo.append((first, then))
    for first, then in todo:
        first.wait()
        then.start()
    for _, then in todo:
        then.wait()


def copy_out(arrays):
    anywhere = pl.BlockSpec(memory_space=pl.ANY)
    sem = pltpu.SemaphoreType.DMA((len(arrays), 4))
    return pl.pallas_call(
        copy_kernel,
        out_shape=tuple(jax.ShapeDtypeStruct(a.shape, a.dtype) for a in arrays),
        in_specs=[anywhere] * len(arrays),
        out_specs=(anywhere,) * len(arrays),
        scratch_shapes=[pltpu.VMEM(a.shape, a.dtype) for a in arrays] + [sem, sem],
        compiler_params=pltpu.CompilerParams(vmem_limit_bytes=60 * MIB),
    )(*arrays)


def local(*args):
    *outs, over = main_call(SIZE, 0, *args)

    def again(state):
        *full, _ = main_call(1024, 1, *args)
        return (jnp.int32(0), *full)

    _, grad_tokens, *grads = lax.while_loop(lambda state: state[0] > 0, again, (over[0], *outs))
    return (grad_tokens, *copy_out(grads))


def solution(mesh):
    in_specs = (
        P(("dp", "mp"), None),
        P(("dp", "mp"), None),
        P(None, "mp"),
        P(None, "mp"),
        P("dp", "mp"),
        P("dp", "mp"),
        P("mp", "dp"),
        P("dp"),
    )
    out_specs = (P(("dp", "mp"), None), P("dp", "mp"), P("dp", "mp"), P("mp", "dp"))
    return jax.shard_map(local, mesh=mesh, in_specs=in_specs, out_specs=out_specs, check_vma=False)
```

```python
import functools

import jax
import jax.numpy as jnp
from jax import lax
from jax.experimental import pallas as pl
from jax.experimental.pallas import tpu as pltpu
from jax.sharding import PartitionSpec as P

SEQ_LEN = 128
NZ, NY = 4, 2
NF = 2
ND = 2
SIZE = 640
BF, F32 = jnp.bfloat16, jnp.float32
MIB = 1 << 20

class Tree:
    def __init__(self, hops=()):
        nodes = [(a, b) for b in (1, 0) for a in (2, 1, 3, 0)][:-1]
        to = {node: (0, 0) for node in nodes}
        to.update(hops)
        self.to, self.nodes = to, sorted(nodes, key=lambda node: (-self.depth(node, to), node[0] != 2))
        self.leaves = [n for n in self.nodes if not self.children(n)]
        self.inner = [n for n in self.nodes if self.children(n)]
        self.levels = max(self.depth(n, to) for n in nodes)

    def depth(self, node, to=None):
        to = to or self.to
        return 0 if node == (0, 0) else 1 + self.depth(to[node], to)

    def children(self, node):
        return [n for n in self.nodes if self.to[n] == node]

    def index(self, node):
        return self.nodes.index(node)


DEEP = Tree(
    hops=(((2, 1), (2, 0)), ((1, 1), (0, 1)), ((3, 1), (0, 1)), ((2, 0), (1, 0)))
)
FLAT = Tree(hops=(((2, 1), (2, 0)), ((1, 1), (0, 1)), ((3, 1), (0, 1))))
ROWS = Tree(hops=(((2, 1), (0, 1)), ((1, 1), (0, 1)), ((3, 1), (0, 1))))
STAR = Tree()
REDUCE = (FLAT, DEEP)
SPREAD = (DEEP, FLAT)
DY_TREE = (FLAT, FLAT)
X_TREE = (ROWS, ROWS)
HOME = (ROWS, FLAT)


class Place:
    def __init__(self):
        self.dp = lax.axis_index("dp")
        self.mp = lax.axis_index("mp")
        self.z, self.yl = self.dp // NY, self.dp % NY
        self.core = self.mp % 2
        self.chip = self.mp // 2
        self.yh, self.x = self.chip // 4, self.chip % 4
        self.sign = 1 - 2 * self.core

    def dp_at(self, da, db):
        z = lax.rem(self.z + self.sign * da + 4, 4)
        return z * NY + (1 - self.yl if db else self.yl)

    def chip_at(self, da, db):
        x = lax.rem(self.x + self.sign * da + 4, 4)
        return (1 - self.yh if db else self.yh) * 4 + x

    def dp_hop(self, src, dst):
        return {"dp": self.dp_at(dst[0] - src[0], src[1] ^ dst[1])}

    def mp_hop(self, src, dst):
        return {"mp": self.chip_at(dst[0] - src[0], src[1] ^ dst[1]) * 2 + self.core}

    def sibling(self):
        return {"mp": self.chip * 2 + 1 - self.core}

    def greet(self):
        sem = pltpu.get_barrier_semaphore()
        peers = [{"dp": lax.rem(self.dp + k, 8)} for k in range(1, 8)]
        peers += [self.sibling()]
        peers += [{"mp": self.chip_at(a, b) * 2 + self.core} for a, b in STAR.nodes]
        for peer in peers:
            pl.semaphore_signal(sem, inc=1, device_id=peer, device_id_type=pl.DeviceIdType.MESH)
        self.peers = len(peers)

    def meet(self):
        pl.semaphore_wait(pltpu.get_barrier_semaphore(), self.peers)


def remote(src, dst, send_sem, recv_sem, device):
    return pltpu.make_async_remote_copy(
        src_ref=src,
        dst_ref=dst,
        send_sem=send_sem,
        recv_sem=recv_sem,
        device_id=device,
        device_id_type=pl.DeviceIdType.MESH,
    )


def send(*args):
    copy = remote(*args)
    copy.start()
    return copy


def dot_nt(a, b):
    return lax.dot_general(a, b, (((1,), (1,)), ((), ())), preferred_element_type=F32)


def dot(a, b):
    return jnp.dot(a, b, preferred_element_type=F32)


class Gather:
    def __init__(self, at, tree, buf, rows, sems):
        self.at, self.tree, self.buf, self.rows = at, tree, buf, rows
        self.send_sem, self.recv_sem, self.sib_send, self.sib_recv = sems
        self.copies = []

    def slab(self, chip, core):
        start = pl.multiple_of((core * 8 + chip) * self.rows, self.rows)
        return self.buf.at[pl.ds(start, self.rows), :]

    def slab_from(self, node):
        return self.slab(self.at.chip_at(-node[0], node[1]), self.at.core)

    def pass_on(self, node):
        ref = self.slab_from(node)
        for child in self.tree.children(node):
            n = self.tree.index(child)
            to = self.at.mp_hop(node, child)
            self.copies.append(send(ref, ref, self.send_sem.at[n], self.recv_sem.at[n], to))
        n = 7 if node == (0, 0) else self.tree.index(node)
        self.copies.append(
            send(ref, ref, self.sib_send.at[n], self.sib_recv.at[n], self.at.sibling())
        )

    def start(self, value):
        start = pl.multiple_of((self.at.core * 8 + self.at.chip) * self.rows, self.rows)
        self.buf[pl.ds(start, self.rows), :] = value
        self.pass_on((0, 0))

    def relay(self, level):
        for node in self.tree.nodes:
            if self.tree.depth(node) == level:
                n = self.tree.index(node)
                arrival(self.slab_from(node), self.send_sem.at[n], self.recv_sem.at[n], self.at)
                self.pass_on(node)

    def finish(self):
        for n, (a, b) in enumerate(self.tree.nodes + [(0, 0)]):
            ref = self.slab(self.at.chip_at(a, b), 1 - self.at.core)
            arrival(ref, self.sib_send.at[n], self.sib_recv.at[n], self.at)

    def drain(self):
        for copy in self.copies:
            copy.wait_send()


def arrival(ref, send_sem, recv_sem, at):
    remote(ref, ref, send_sem, recv_sem, at.sibling()).wait_recv()


def live_rows(length, parity):
    rest = length & 15
    extra = jnp.where(parity == 0, jnp.minimum(rest, 8), jnp.maximum(rest - 8, 0))
    return (length >> 4) * 8 + extra


def rank_of(index, lens, h, slabs):
    if slabs:
        slab = index >> 5
        core = slab >> 3
        response = ((index >> 3) & 3) * 2 + ((core + h) & 1)
        place = ((slab & 7) * 2 + core) * 8 + (index & 7)
    else:
        response = index >> 7
        place = index & 127
    rank = jnp.full(index.shape, -1, jnp.int32)
    first = 0
    for r in range(8):
        parity = (r + h) & 1
        live = (response == r) & (place < lens[r]) & (((place >> 3) & 1) == parity)
        rank = jnp.where(live, (place >> 4) * 8 + (place & 7) + first, rank)
        first = first + live_rows(lens[r], parity)
    return rank


def fold(value):
    mid = value.shape[1] // 2
    return jnp.concatenate([value[:, :mid], value[:, mid:]], axis=0)


def main_kernel(
    tok_hbm,
    grad_hbm,
    length,
    gp,
    up,
    wg_hbm,
    wu_hbm,
    wd_hbm,
    gt_out,
    gg_out,
    gu_out,
    gd_out,
    over_out,
    tok,
    grad,
    sbuf,
    rbuf,
    sbuf_x,
    rbuf_x,
    dyb,
    xb,
    p_slab,
    p_own,
    p_back,
    dyc,
    wg,
    wu,
    act,
    hid,
    dact,
    term,
    rs_out,
    rs_in,
    dh,
    half_out,
    half_in,
    mp_out,
    mp_in,
    fin_out,
    fin_in,
    in_sem,
    a_send,
    a_recv,
    ax_send,
    ax_recv,
    w_sem,
    raw_sem,
    rs_send,
    rs_recv,
    ag_send,
    ag_recv,
    dy_send,
    dy_recv,
    dys_send,
    dys_recv,
    x_send,
    x_recv,
    xs_send,
    xs_recv,
    h_send,
    h_recv,
    m_send,
    m_recv,
    f_send,
    f_recv,
):
    at = Place()
    cap = dyc.shape[0] // 2
    rows = cap // 8
    fw = term.shape[3]
    dl = dyc.shape[1]
    dw = dl // ND
    sent = []

    loads = [
        pltpu.make_async_copy(src, dst, in_sem.at[n])
        for n, (src, dst) in enumerate(((tok_hbm, tok), (grad_hbm, grad)))
    ]
    for copy in loads:
        copy.start()
    at.greet()
    own_len = jnp.full((16, 128), length[0], jnp.int32).astype(F32).astype(BF)
    loads[1].wait()
    for c in range(8):
        sbuf[c, :, :dw] = fold(grad[:, c * dl : (c + 1) * dl].astype(F32)).astype(BF)
        sbuf[c, :, dw:] = own_len
    at.meet()

    def to_dp(src, dst, send_sem, recv_sem):
        for k in (4, 3, 5, 2, 6, 1, 7):
            peer = lax.rem(at.dp + k, 8)
            sent.append(
                send(src.at[peer], dst.at[at.dp], send_sem.at[k], recv_sem.at[k], {"dp": peer})
            )
        dst[at.dp] = src[at.dp]

    def from_dp(dst, send_sem, recv_sem):
        for k in (4, 3, 5, 2, 6, 1, 7):
            source = lax.rem(at.dp + 8 - k, 8)
            arrival(dst.at[source], send_sem.at[k], recv_sem.at[k], at)

    to_dp(sbuf, rbuf, a_send, a_recv)
    loads[0].wait()
    for c in range(8):
        sbuf_x[c] = fold(tok[:, c * dl : (c + 1) * dl].astype(F32)).astype(BF)

    def piece(j):
        return pl.ds(pl.multiple_of(j * fw, fw), fw)

    weights = [pltpu.make_async_copy(wd_hbm, gd_out, w_sem.at[0])]
    for j in range(NF):
        for n, (src, dst) in enumerate(((wg_hbm, wg), (wu_hbm, wu))):
            sem = w_sem.at[1 + 2 * j + n]
            weights.append(pltpu.make_async_copy(src.at[:, piece(j)], dst.at[j], sem))
    raws = [
        pltpu.make_async_copy(src, dst, raw_sem.at[n])
        for n, (src, dst) in enumerate(((gp, gg_out), (up, gu_out)))
    ]
    weights[0].start()
    for copy in raws:
        copy.start()
    from_dp(rbuf, a_send, a_recv)

    def slab_of(buf, h):
        parity = (at.core + h) & 1
        blocks = []
        for k in range(4):
            value = buf[2 * k + parity].astype(F32)
            blocks.append(jnp.concatenate([value[:8, :dw], value[8:, :dw]], axis=1))
        return jnp.concatenate(blocks, axis=0).astype(BF)

    def one_hot(ref, slot, h, slabs):
        size = ref.shape[2]
        rank = rank_of(lax.broadcasted_iota(jnp.int32, (1, size), 1), lens, h, slabs)
        blk = 64

        @pl.loop(0, cap // blk)
        def _(i):
            start = pl.multiple_of(i * blk, blk)
            index = lax.broadcasted_iota(jnp.int32, (blk, size), 0) + start
            ref[slot, pl.ds(start, blk), :] = jnp.where(index == rank, 1.0, 0.0).astype(BF)

    def back_matrix(h):
        blk = 128

        @pl.loop(0, 512 // blk)
        def _(i):
            start = pl.multiple_of(i * blk, blk)
            index = lax.broadcasted_iota(jnp.int32, (blk, 1), 0) + start
            rank = rank_of(index, lens, h, True)
            lane = lax.broadcasted_iota(jnp.int32, (blk, cap), 1)
            p_back[pl.ds(start, blk), :] = jnp.where(lane == rank, 1.0, 0.0).astype(BF)

    gather_dy, gather_x = [], []
    for h in range(2):
        sems = [sem.at[h] for sem in (dy_send, dy_recv, dys_send, dys_recv)]
        gather_dy.append(Gather(at, DY_TREE[h], dyb.at[h], 32, sems))
        sems = [sem.at[h] for sem in (x_send, x_recv, xs_send, xs_recv)]
        gather_x.append(Gather(at, X_TREE[h], xb.at[h], 32, sems))
    gather_dy[0].start(slab_of(rbuf, 0))
    to_dp(sbuf_x, rbuf_x, ax_send, ax_recv)
    lens = [jnp.max(rbuf[r].astype(F32)[0:1, dw:]).astype(jnp.int32) for r in range(8)]
    need = [sum(live_rows(lens[r], (r + h) & 1) for r in range(8)) for h in range(2)]
    over_out[0] = (jnp.maximum(need[0], need[1]) > cap).astype(jnp.int32)

    def half_rows(h):
        return slice(h * cap, (h + 1) * cap)

    def chunk(h, j, offset):
        owner = at.dp_at(-offset[0], offset[1])
        return fold(term[h, j, pl.ds(pl.multiple_of(owner * rows, rows), rows), :])

    def rs_copy(h, j, node):
        e = REDUCE[h].index(node)
        return remote(
            rs_out.at[h, j, e],
            rs_in.at[h, j, e],
            rs_send.at[h, j, e],
            rs_recv.at[h, j, e],
            at.dp_hop(node, REDUCE[h].to[node]),
        )

    def rs_sum(h, j, node):
        value = chunk(h, j, node)
        for child in REDUCE[h].children(node):
            e = REDUCE[h].index(child)
            arrival(rs_in.at[h, j, e], rs_send.at[h, j, e], rs_recv.at[h, j, e], at)
            value = value + rs_in[h, j, e].astype(F32)
        return value

    def rs_hop(h, j, node):
        rs_out[h, j, REDUCE[h].index(node)] = rs_sum(h, j, node).astype(BF)
        rs_copy(h, j, node).start()

    def terms(h):
        dyc[half_rows(h), :] = dot(p_slab[h], dyb[h]).astype(BF)
        if h == 0:
            weights[0].wait()

        @pl.loop(0, NF)
        def _(j):
            term[h, j] = dot_nt(dyc[half_rows(h), :], gd_out[piece(j), :])
            for node in REDUCE[h].leaves:
                rs_hop(h, j, node)

    def rs_inner(h, n):
        @pl.loop(0, NF)
        def _(j):
            for node in REDUCE[h].inner[n : n + 1]:
                rs_hop(h, j, node)

    def ag_ref(h, j, offset):
        return dh.at[h, j, at.dp_at(-offset[0], offset[1])]

    def ag_copy(h, j, node):
        e = SPREAD[h].index(node)
        ref = ag_ref(h, j, SPREAD[h].to[node])
        to = at.dp_hop(SPREAD[h].to[node], node)
        return remote(ref, ref, ag_send.at[h, j, e], ag_recv.at[h, j, e], to)

    def ag_arrive(h, j, node):
        e = SPREAD[h].index(node)
        arrival(ag_ref(h, j, node), ag_send.at[h, j, e], ag_recv.at[h, j, e], at)

    def ag_pass_on(h, j, node):
        for child in SPREAD[h].children(node):
            ag_copy(h, j, child).start()

    def rs_own(h):
        @pl.loop(0, NF)
        def _(j):
            dh[h, j, at.dp] = rs_sum(h, j, (0, 0)).astype(BF)
            ag_pass_on(h, j, (0, 0))

    def ag_forward(h, level):
        @pl.loop(0, NF)
        def _(j):
            for node in SPREAD[h].inner:
                if SPREAD[h].depth(node) == level:
                    ag_arrive(h, j, node)
                    ag_pass_on(h, j, node)

    def pack(h, which):
        if h == 0:
            raws[which].wait()

        @pl.loop(0, NF)
        def _(j):
            value = dot(p_own[0], (gg_out, gu_out)[which][:, piece(j)])
            for o in range(8):
                act[h, 2 * j + which, o] = fold(value[o * rows : (o + 1) * rows, :]).astype(BF)

    def unfold_store(ref, h, j, k, pair):
        here = pl.ds(pl.multiple_of(h * cap + k * 2 * rows, 16), 2 * rows)
        mid = fw // 2
        for n in range(2):
            part = [v[n * rows : (n + 1) * rows, :] for v in pair]
            ref[j, here, n * mid : (n + 1) * mid] = jnp.concatenate(part, axis=0).astype(BF)

    def hidden(h):
        @pl.loop(0, 4 * NF)
        def _(i):
            j, k = i // 4, i % 4
            pair = []
            for n in range(2):
                g = act[h, 2 * j, 2 * k + n].astype(F32)
                u = act[h, 2 * j + 1, 2 * k + n].astype(F32)
                pair.append(g * jax.nn.sigmoid(g) * u)
            unfold_store(hid, h, j, k, pair)

    def gate_backward(h, j):
        @pl.loop(0, 4)
        def _(k):
            gates, ups = [], []
            for n in range(2):
                g = act[h, 2 * j, 2 * k + n].astype(F32)
                u = act[h, 2 * j + 1, 2 * k + n].astype(F32)
                d = dh[h, j, 2 * k + n].astype(F32)
                sig = jax.nn.sigmoid(g)
                gates.append(d * u * sig * (1.0 + g * (1.0 - sig)))
                ups.append(d * g * sig)
            unfold_store(dact, h, 2 * j, k, gates)
            unfold_store(dact, h, 2 * j + 1, k, ups)

    def half_copy(h, d):
        return remote(
            half_out.at[h, d], half_in.at[h, d], h_send.at[h, d], h_recv.at[h, d], at.sibling()
        )

    def unpack(h, d, core):
        value = term[h, d, :, :dw]
        high = value.astype(BF)
        low = (value - high.astype(F32)).astype(BF)
        back = p_back[pl.ds(pl.multiple_of(core * 256, 256), 256), :]
        return dot(back, high) + dot(back, low)

    def parts(h):
        here = half_rows(h)
        if h == 0:
            for copy in weights[1:]:
                copy.wait()

        def arrived(j):
            for node in reversed(SPREAD[h].leaves):
                ag_arrive(h, j, node)
            gate_backward(h, j)

        def part(j, d):
            units = pl.ds(pl.multiple_of(d * dw, dw), dw)
            value = dot_nt(dact[2 * j, here, :], wg[j, units, :])
            return value + dot_nt(dact[2 * j + 1, here, :], wu[j, units, :])

        for j in range(NF - 1):
            arrived(j)

            @pl.loop(0, ND)
            def _(d):
                value = part(j, d)
                term[h, d, :, :dw] = value + term[h, d, :, :dw] if j else value

        arrived(NF - 1)

        @pl.loop(0, ND)
        def _(d):
            term[h, d, :, :dw] = term[h, d, :, :dw] + part(NF - 1, d)
            half_out[h, d] = unpack(h, d, 1 - at.core).astype(BF)
            half_copy(h, d).start()

    def mp_chunk(h, d, offset):
        owner = at.chip_at(-offset[0], offset[1])
        return term[h, d, pl.ds(pl.multiple_of(owner * 32, 32), 32), :dw]

    def mp_copy(h, d, node):
        e = HOME[h].index(node)
        return remote(
            mp_out.at[h, d, e],
            mp_in.at[h, d, e],
            m_send.at[h, d, e],
            m_recv.at[h, d, e],
            at.mp_hop(node, HOME[h].to[node]),
        )

    def mp_sum(h, d, node):
        value = mp_chunk(h, d, node)
        for child in HOME[h].children(node):
            e = HOME[h].index(child)
            arrival(mp_in.at[h, d, e], m_send.at[h, d, e], m_recv.at[h, d, e], at)
            value = value + mp_in[h, d, e].astype(F32)
        return value

    def mp_hop(h, d, node):
        mp_out[h, d, HOME[h].index(node)] = mp_sum(h, d, node).astype(BF)
        mp_copy(h, d, node).start()

    def mp_leaves(h):
        @pl.loop(0, ND)
        def _(d):
            value = unpack(h, d, at.core)
            half_copy(h, d).wait_recv()
            term[h, d, :256, :dw] = value + half_in[h, d].astype(F32)
            for node in HOME[h].leaves:
                mp_hop(h, d, node)

    def mp_inner(h):
        if HOME[h].inner:

            @pl.loop(0, ND)
            def _(d):
                for node in HOME[h].inner:
                    mp_hop(h, d, node)

    def mp_own(h):
        sums = [mp_sum(h, d, (0, 0)) for d in range(ND)]
        for k in range(4):
            both = jnp.concatenate([s[k * 8 : k * 8 + 8, :] for s in sums], axis=0)
            fin_out[2 * k + ((at.core + h) & 1)] = both.astype(BF)

    def tn(a, b):
        return lax.dot_general(a, b, (((0,), (0,)), ((), ())), preferred_element_type=F32).astype(BF)

    def weight_grad(j):
        for n, out in enumerate((gg_out, gu_out)):
            out[:, piece(j)] = tn(dyc[...], dact[2 * j + n])

    def down_grads():
        @pl.loop(0, NF)
        def _(j):
            gd_out[piece(j), :] = tn(hid[j], dyc[...])

    a, b = 0, 1
    one_hot(p_slab, a, a, True)
    one_hot(p_own, 0, a, False)
    pack(a, 0)
    gather_dy[b].start(slab_of(rbuf, b))
    for copy in weights[1:]:
        copy.start()
    pack(a, 1)
    one_hot(p_slab, b, b, True)
    for level in range(1, DY_TREE[a].levels + 1):
        gather_dy[a].relay(level)
    gather_dy[b].relay(1)
    gather_dy[a].finish()
    terms(a)
    for level in range(2, DY_TREE[b].levels + 1):
        gather_dy[b].relay(level)
    one_hot(p_own, 0, b, False)
    rs_inner(a, 0)
    gather_dy[b].finish()
    rs_inner(a, 1)
    terms(b)
    rs_inner(a, 2)
    from_dp(rbuf_x, ax_send, ax_recv)
    for h in range(2):
        gather_x[h].start(slab_of(rbuf_x, h))
    pack(b, 0)
    rs_own(a)
    rs_inner(b, 0)
    rs_inner(b, 1)
    pack(b, 1)
    rs_inner(b, 2)
    hidden(a)
    ag_forward(a, 1)
    hidden(b)
    rs_own(b)
    ag_forward(a, 2)
    for h in range(2):
        gather_x[h].relay(1)
    down_grads()
    ag_forward(b, 1)
    back_matrix(a)
    parts(a)
    ag_forward(b, 2)
    for h in range(2):
        gather_x[h].relay(2)
    mp_leaves(a)
    back_matrix(b)
    for h in range(2):
        gather_x[h].finish()
        dyc[half_rows(h), :] = dot(p_slab[h], xb[h]).astype(BF)
    parts(b)
    mp_inner(a)
    mp_leaves(b)
    mp_own(a)

    def weight_grads(first, last):
        @pl.loop(first, last)
        def _(j):
            weight_grad(j)

    mp_inner(b)
    weight_grads(0, 1)
    mp_own(b)
    to_dp(fin_out, fin_in, f_send, f_recv)
    weight_grads(1, NF)
    for gather in gather_dy + gather_x:
        gather.drain()

    for h in range(2):

        @pl.loop(0, NF)
        def _(j):
            for node in STAR.nodes:
                rs_copy(h, j, node).wait_send()
                ag_copy(h, j, node).wait_send()

        @pl.loop(0, ND)
        def _(d):
            half_copy(h, d).wait_send()
            for node in STAR.nodes:
                mp_copy(h, d, node).wait_send()

    from_dp(fin_in, f_send, f_recv)
    for c in range(8):
        both = fin_in[c].astype(F32)
        for d in range(ND):
            gt_out[:, c * dl + d * dw : c * dl + (d + 1) * dw] = both[d * 8 : d * 8 + 8, :].astype(BF)
    for copy in sent:
        copy.wait_send()


def main_call(size, number, tokens, out_grad, gate_pre, up_pre, wg, wu, wd, lengths):
    dl, fl = tokens.shape[1] // 8, gate_pre.shape[1]
    fw, dw, cap, rows = fl // NF, dl // ND, size // 2, size // 16
    dma = pltpu.SemaphoreType.DMA
    vmem, smem = pl.BlockSpec(memory_space=pltpu.VMEM), pl.BlockSpec(memory_space=pltpu.SMEM)
    anywhere = pl.BlockSpec(memory_space=pl.ANY)
    buffers = [
        (tokens.shape, BF),
        (tokens.shape, BF),
        ((8, 16, dw + 128), BF),
        ((8, 16, dw + 128), BF),
        ((8, 16, dw), BF),
        ((8, 16, dw), BF),
        ((2, 512, dl), BF),
        ((2, 512, dl), BF),
        ((2, cap, 512), BF),
        ((1, cap, 1024), BF),
        ((512, cap), BF),
        ((size, dl), BF),
        ((NF, dl, fw), BF),
        ((NF, dl, fw), BF),
        ((2, 2 * NF, 8, 2 * rows, fw // 2), BF),
        ((NF, size, fw), BF),
        ((2 * NF, size, fw), BF),
        ((2, NF, cap, fw), F32),
        ((2, NF, 7, 2 * rows, fw // 2), BF),
        ((2, NF, 7, 2 * rows, fw // 2), BF),
        ((2, NF, 8, 2 * rows, fw // 2), BF),
        ((2, ND, 256, dw), BF),
        ((2, ND, 256, dw), BF),
        ((2, ND, 7, 32, dw), BF),
        ((2, ND, 7, 32, dw), BF),
        ((8, 16, dw), BF),
        ((8, 16, dw), BF),
    ]
    sems = [(2,), (8,), (8,), (8,), (8,), (1 + 2 * NF,), (2,)]
    sems += [(2, NF, 7)] * 4
    sems += [(2, 7), (2, 7), (2, 8), (2, 8)] * 2
    sems += [(2, ND), (2, ND), (2, ND, 7), (2, ND, 7), (8,), (8,)]
    return pl.pallas_call(
        main_kernel,
        out_shape=(
            jax.ShapeDtypeStruct((8, dl * 8), BF),
            jax.ShapeDtypeStruct((dl, fl), BF),
            jax.ShapeDtypeStruct((dl, fl), BF),
            jax.ShapeDtypeStruct((fl, dl), BF),
            jax.ShapeDtypeStruct((1,), jnp.int32),
        ),
        in_specs=[anywhere, anywhere, smem] + [anywhere] * 5,
        out_specs=(vmem,) * 4 + (smem,),
        scratch_shapes=[pltpu.VMEM(s, t) for s, t in buffers] + [dma(s) for s in sems],
        compiler_params=pltpu.CompilerParams(
            collective_id=number, has_side_effects=True, vmem_limit_bytes=(38 if size <= SIZE else 63) * MIB
        ),
    )(tokens, out_grad, lengths, gate_pre, up_pre, wg, wu, wd)


def copy_kernel(*refs):
    sem, refs = refs[-1], refs[:-1]
    count = len(refs) // 2
    copies = [
        pltpu.make_async_copy(refs[n], refs[count + n], sem.at[n]) for n in range(count)
    ]
    for copy in copies:
        copy.start()
    for copy in copies:
        copy.wait()


def copy_out(arrays):
    anywhere = pl.BlockSpec(memory_space=pl.ANY)
    return pl.pallas_call(
        copy_kernel,
        out_shape=tuple(jax.ShapeDtypeStruct(a.shape, a.dtype) for a in arrays),
        in_specs=[pl.BlockSpec(memory_space=pltpu.VMEM)] * len(arrays),
        out_specs=(anywhere,) * len(arrays),
        scratch_shapes=[pltpu.SemaphoreType.DMA((len(arrays),))],
        compiler_params=pltpu.CompilerParams(vmem_limit_bytes=24 * MIB),
    )(*arrays)


def local(*args):
    *outs, over = main_call(SIZE, 0, *args)

    def again(state):
        *full, _ = main_call(1024, 1, *args)
        return (jnp.int32(0), *copy_out(full))

    state = (over[0], *copy_out(outs))
    return lax.while_loop(lambda state: state[0] > 0, again, state)[1:]


def solution(mesh):
    in_specs = (
        P(("dp", "mp"), None),
        P(("dp", "mp"), None),
        P(None, "mp"),
        P(None, "mp"),
        P("dp", "mp"),
        P("dp", "mp"),
        P("mp", "dp"),
        P("dp"),
    )
    out_specs = (P(("dp", "mp"), None), P("dp", "mp"), P("dp", "mp"), P("mp", "dp"))
    return jax.shard_map(local, mesh=mesh, in_specs=in_specs, out_specs=out_specs, check_vma=False)
```

```python
import functools

import jax
import jax.numpy as jnp
from jax import lax
from jax.experimental import pallas as pl
from jax.experimental.pallas import tpu as pltpu
from jax.sharding import PartitionSpec as P

SEQ_LEN = 128
NZ, NY = 4, 2
NF = 2
ND = 2
SIZE = 640
BF, F32 = jnp.bfloat16, jnp.float32
MIB = 1 << 20

class Tree:
    def __init__(self, hops=()):
        nodes = [(a, b) for b in (1, 0) for a in (2, 1, 3, 0)][:-1]
        to = {node: (0, 0) for node in nodes}
        to.update(hops)
        self.to, self.nodes = to, sorted(nodes, key=lambda node: (-self.depth(node, to), node[0] != 2))
        self.leaves = [n for n in self.nodes if not self.children(n)]
        self.inner = [n for n in self.nodes if self.children(n)]
        self.levels = max(self.depth(n, to) for n in nodes)

    def depth(self, node, to=None):
        to = to or self.to
        return 0 if node == (0, 0) else 1 + self.depth(to[node], to)

    def children(self, node):
        return [n for n in self.nodes if self.to[n] == node]

    def index(self, node):
        return self.nodes.index(node)


DEEP = Tree(
    hops=(((2, 1), (2, 0)), ((1, 1), (0, 1)), ((3, 1), (0, 1)), ((2, 0), (1, 0)))
)
FLAT = Tree(hops=(((2, 1), (2, 0)), ((1, 1), (0, 1)), ((3, 1), (0, 1))))
ROWS = Tree(hops=(((2, 1), (0, 1)), ((1, 1), (0, 1)), ((3, 1), (0, 1))))
STAR = Tree()
REDUCE = (FLAT, DEEP)
SPREAD = (DEEP, FLAT)
DY_TREE = (FLAT, FLAT)
X_TREE = (ROWS, ROWS)
HOME = (ROWS, FLAT)


class Place:
    def __init__(self):
        self.dp = lax.axis_index("dp")
        self.mp = lax.axis_index("mp")
        self.z, self.yl = self.dp // NY, self.dp % NY
        self.core = self.mp % 2
        self.chip = self.mp // 2
        self.yh, self.x = self.chip // 4, self.chip % 4
        self.sign = 1 - 2 * self.core

    def dp_at(self, da, db):
        z = lax.rem(self.z + self.sign * da + 4, 4)
        return z * NY + (1 - self.yl if db else self.yl)

    def chip_at(self, da, db):
        x = lax.rem(self.x + self.sign * da + 4, 4)
        return (1 - self.yh if db else self.yh) * 4 + x

    def dp_hop(self, src, dst):
        return {"dp": self.dp_at(dst[0] - src[0], src[1] ^ dst[1])}

    def mp_hop(self, src, dst):
        return {"mp": self.chip_at(dst[0] - src[0], src[1] ^ dst[1]) * 2 + self.core}

    def sibling(self):
        return {"mp": self.chip * 2 + 1 - self.core}

    def greet(self):
        sem = pltpu.get_barrier_semaphore()
        peers = [{"dp": lax.rem(self.dp + k, 8)} for k in range(1, 8)]
        peers += [self.sibling()]
        peers += [{"mp": self.chip_at(a, b) * 2 + self.core} for a, b in STAR.nodes]
        for peer in peers:
            pl.semaphore_signal(sem, inc=1, device_id=peer, device_id_type=pl.DeviceIdType.MESH)
        self.peers = len(peers)

    def meet(self):
        pl.semaphore_wait(pltpu.get_barrier_semaphore(), self.peers)


def remote(src, dst, send_sem, recv_sem, device):
    return pltpu.make_async_remote_copy(
        src_ref=src,
        dst_ref=dst,
        send_sem=send_sem,
        recv_sem=recv_sem,
        device_id=device,
        device_id_type=pl.DeviceIdType.MESH,
    )


def send(*args):
    copy = remote(*args)
    copy.start()
    return copy


def dot_nt(a, b):
    return lax.dot_general(a, b, (((1,), (1,)), ((), ())), preferred_element_type=F32)


def dot(a, b):
    return jnp.dot(a, b, preferred_element_type=F32)


class Gather:
    def __init__(self, at, tree, buf, rows, sems):
        self.at, self.tree, self.buf, self.rows = at, tree, buf, rows
        self.send_sem, self.recv_sem, self.sib_send, self.sib_recv = sems
        self.copies = []

    def slab(self, chip, core):
        start = pl.multiple_of((core * 8 + chip) * self.rows, self.rows)
        return self.buf.at[pl.ds(start, self.rows), :]

    def slab_from(self, node):
        return self.slab(self.at.chip_at(-node[0], node[1]), self.at.core)

    def pass_on(self, node):
        ref = self.slab_from(node)
        for child in self.tree.children(node):
            n = self.tree.index(child)
            to = self.at.mp_hop(node, child)
            self.copies.append(send(ref, ref, self.send_sem.at[n], self.recv_sem.at[n], to))
        n = 7 if node == (0, 0) else self.tree.index(node)
        self.copies.append(
            send(ref, ref, self.sib_send.at[n], self.sib_recv.at[n], self.at.sibling())
        )

    def start(self, value):
        start = pl.multiple_of((self.at.core * 8 + self.at.chip) * self.rows, self.rows)
        self.buf[pl.ds(start, self.rows), :] = value
        self.pass_on((0, 0))

    def relay(self, level):
        for node in self.tree.nodes:
            if self.tree.depth(node) == level:
                n = self.tree.index(node)
                arrival(self.slab_from(node), self.send_sem.at[n], self.recv_sem.at[n], self.at)
                self.pass_on(node)

    def finish(self):
        for n, (a, b) in enumerate(self.tree.nodes + [(0, 0)]):
            ref = self.slab(self.at.chip_at(a, b), 1 - self.at.core)
            arrival(ref, self.sib_send.at[n], self.sib_recv.at[n], self.at)

    def drain(self):
        for copy in self.copies:
            copy.wait_send()


def arrival(ref, send_sem, recv_sem, at):
    remote(ref, ref, send_sem, recv_sem, at.sibling()).wait_recv()


def live_rows(length, parity):
    rest = length & 15
    extra = jnp.where(parity == 0, jnp.minimum(rest, 8), jnp.maximum(rest - 8, 0))
    return (length >> 4) * 8 + extra


def rank_of(index, lens, h, slabs):
    if slabs:
        slab = index >> 5
        core = slab >> 3
        response = ((index >> 3) & 3) * 2 + ((core + h) & 1)
        place = ((slab & 7) * 2 + core) * 8 + (index & 7)
    else:
        response = index >> 7
        place = index & 127
    rank = jnp.full(index.shape, -1, jnp.int32)
    first = 0
    for r in range(8):
        parity = (r + h) & 1
        live = (response == r) & (place < lens[r]) & (((place >> 3) & 1) == parity)
        rank = jnp.where(live, (place >> 4) * 8 + (place & 7) + first, rank)
        first = first + live_rows(lens[r], parity)
    return rank


def fold(value):
    mid = value.shape[1] // 2
    return jnp.concatenate([value[:, :mid], value[:, mid:]], axis=0)


def main_kernel(
    tok_hbm,
    grad_hbm,
    length,
    gp,
    up,
    wg_hbm,
    wu_hbm,
    wd_hbm,
    gt_out,
    gg_out,
    gu_out,
    gd_out,
    over_out,
    tok,
    grad,
    sbuf,
    rbuf,
    sbuf_x,
    rbuf_x,
    dyb,
    xb,
    p_slab,
    p_own,
    p_back,
    dyc,
    wg,
    wu,
    act,
    hid,
    dact,
    term,
    rs_out,
    rs_in,
    dh,
    half_out,
    half_in,
    mp_out,
    mp_in,
    fin_out,
    fin_in,
    in_sem,
    a_send,
    a_recv,
    ax_send,
    ax_recv,
    w_sem,
    raw_sem,
    rs_send,
    rs_recv,
    ag_send,
    ag_recv,
    dy_send,
    dy_recv,
    dys_send,
    dys_recv,
    x_send,
    x_recv,
    xs_send,
    xs_recv,
    h_send,
    h_recv,
    m_send,
    m_recv,
    f_send,
    f_recv,
):
    at = Place()
    cap = dyc.shape[0] // 2
    rows = cap // 8
    fw = term.shape[3]
    dl = dyc.shape[1]
    dw = dl // ND
    sent = []

    loads = [
        pltpu.make_async_copy(src, dst, in_sem.at[n])
        for n, (src, dst) in enumerate(((tok_hbm, tok), (grad_hbm, grad)))
    ]
    for copy in loads:
        copy.start()
    at.greet()
    own_len = jnp.full((16, 128), length[0], jnp.int32).astype(F32).astype(BF)
    loads[1].wait()
    for c in range(8):
        sbuf[c, :, :dw] = fold(grad[:, c * dl : (c + 1) * dl].astype(F32)).astype(BF)
        sbuf[c, :, dw:] = own_len
    at.meet()

    def to_dp(src, dst, send_sem, recv_sem):
        for k in (4, 3, 5, 2, 6, 1, 7):
            peer = lax.rem(at.dp + k, 8)
            sent.append(
                send(src.at[peer], dst.at[at.dp], send_sem.at[k], recv_sem.at[k], {"dp": peer})
            )
        dst[at.dp] = src[at.dp]

    def from_dp(dst, send_sem, recv_sem):
        for k in (4, 3, 5, 2, 6, 1, 7):
            source = lax.rem(at.dp + 8 - k, 8)
            arrival(dst.at[source], send_sem.at[k], recv_sem.at[k], at)

    to_dp(sbuf, rbuf, a_send, a_recv)
    loads[0].wait()
    for c in range(8):
        sbuf_x[c] = fold(tok[:, c * dl : (c + 1) * dl].astype(F32)).astype(BF)

    def piece(j):
        return pl.ds(pl.multiple_of(j * fw, fw), fw)

    weights = [pltpu.make_async_copy(wd_hbm, gd_out, w_sem.at[0])]
    for j in range(NF):
        for n, (src, dst) in enumerate(((wg_hbm, wg), (wu_hbm, wu))):
            sem = w_sem.at[1 + 2 * j + n]
            weights.append(pltpu.make_async_copy(src.at[:, piece(j)], dst.at[j], sem))
    raws = [
        pltpu.make_async_copy(src, dst, raw_sem.at[n])
        for n, (src, dst) in enumerate(((gp, gg_out), (up, gu_out)))
    ]
    weights[0].start()
    for copy in raws:
        copy.start()
    from_dp(rbuf, a_send, a_recv)

    def slab_of(buf, h):
        parity = (at.core + h) & 1
        blocks = []
        for k in range(4):
            value = buf[2 * k + parity].astype(F32)
            blocks.append(jnp.concatenate([value[:8, :dw], value[8:, :dw]], axis=1))
        return jnp.concatenate(blocks, axis=0).astype(BF)

    def one_hot(ref, slot, h, slabs):
        size = ref.shape[2]
        rank = rank_of(lax.broadcasted_iota(jnp.int32, (1, size), 1), lens, h, slabs)
        blk = 64

        @pl.loop(0, cap // blk)
        def _(i):
            start = pl.multiple_of(i * blk, blk)
            index = lax.broadcasted_iota(jnp.int32, (blk, size), 0) + start
            ref[slot, pl.ds(start, blk), :] = jnp.where(index == rank, 1.0, 0.0).astype(BF)

    def back_matrix(h):
        blk = 128

        @pl.loop(0, 512 // blk)
        def _(i):
            start = pl.multiple_of(i * blk, blk)
            index = lax.broadcasted_iota(jnp.int32, (blk, 1), 0) + start
            rank = rank_of(index, lens, h, True)
            lane = lax.broadcasted_iota(jnp.int32, (blk, cap), 1)
            p_back[pl.ds(start, blk), :] = jnp.where(lane == rank, 1.0, 0.0).astype(BF)

    gather_dy, gather_x = [], []
    for h in range(2):
        sems = [sem.at[h] for sem in (dy_send, dy_recv, dys_send, dys_recv)]
        gather_dy.append(Gather(at, DY_TREE[h], dyb.at[h], 32, sems))
        sems = [sem.at[h] for sem in (x_send, x_recv, xs_send, xs_recv)]
        gather_x.append(Gather(at, X_TREE[h], xb.at[h], 32, sems))
    gather_dy[0].start(slab_of(rbuf, 0))
    to_dp(sbuf_x, rbuf_x, ax_send, ax_recv)
    lens = [jnp.max(rbuf[r].astype(F32)[0:1, dw:]).astype(jnp.int32) for r in range(8)]
    need = [sum(live_rows(lens[r], (r + h) & 1) for r in range(8)) for h in range(2)]
    over_out[0] = (jnp.maximum(need[0], need[1]) > cap).astype(jnp.int32)

    def half_rows(h):
        return slice(h * cap, (h + 1) * cap)

    def chunk(h, j, offset):
        owner = at.dp_at(-offset[0], offset[1])
        return fold(term[h, j, pl.ds(pl.multiple_of(owner * rows, rows), rows), :])

    def rs_copy(h, j, node):
        e = REDUCE[h].index(node)
        return remote(
            rs_out.at[h, j, e],
            rs_in.at[h, j, e],
            rs_send.at[h, j, e],
            rs_recv.at[h, j, e],
            at.dp_hop(node, REDUCE[h].to[node]),
        )

    def rs_sum(h, j, node):
        value = chunk(h, j, node)
        for child in REDUCE[h].children(node):
            e = REDUCE[h].index(child)
            arrival(rs_in.at[h, j, e], rs_send.at[h, j, e], rs_recv.at[h, j, e], at)
            value = value + rs_in[h, j, e].astype(F32)
        return value

    def rs_hop(h, j, node):
        rs_out[h, j, REDUCE[h].index(node)] = rs_sum(h, j, node).astype(BF)
        rs_copy(h, j, node).start()

    def terms(h):
        dyc[half_rows(h), :] = dot(p_slab[h], dyb[h]).astype(BF)
        if h == 0:
            weights[0].wait()

        @pl.loop(0, NF)
        def _(j):
            term[h, j] = dot_nt(dyc[half_rows(h), :], gd_out[piece(j), :])
            for node in REDUCE[h].leaves:
                rs_hop(h, j, node)

    def rs_inner(h, n):
        @pl.loop(0, NF)
        def _(j):
            for node in REDUCE[h].inner[n : n + 1]:
                rs_hop(h, j, node)

    def ag_ref(h, j, offset):
        return dh.at[h, j, at.dp_at(-offset[0], offset[1])]

    def ag_copy(h, j, node):
        e = SPREAD[h].index(node)
        ref = ag_ref(h, j, SPREAD[h].to[node])
        to = at.dp_hop(SPREAD[h].to[node], node)
        return remote(ref, ref, ag_send.at[h, j, e], ag_recv.at[h, j, e], to)

    def ag_arrive(h, j, node):
        e = SPREAD[h].index(node)
        arrival(ag_ref(h, j, node), ag_send.at[h, j, e], ag_recv.at[h, j, e], at)

    def ag_pass_on(h, j, node):
        for child in SPREAD[h].children(node):
            ag_copy(h, j, child).start()

    def rs_own(h):
        @pl.loop(0, NF)
        def _(j):
            dh[h, j, at.dp] = rs_sum(h, j, (0, 0)).astype(BF)
            ag_pass_on(h, j, (0, 0))

    def ag_forward(h, level):
        @pl.loop(0, NF)
        def _(j):
            for node in SPREAD[h].inner:
                if SPREAD[h].depth(node) == level:
                    ag_arrive(h, j, node)
                    ag_pass_on(h, j, node)

    def pack(h, which):
        if h == 0:
            raws[which].wait()

        @pl.loop(0, NF)
        def _(j):
            value = dot(p_own[0], (gg_out, gu_out)[which][:, piece(j)])
            for o in range(8):
                act[h, 2 * j + which, o] = fold(value[o * rows : (o + 1) * rows, :]).astype(BF)

    def unfold_store(ref, h, j, k, pair):
        here = pl.ds(pl.multiple_of(h * cap + k * 2 * rows, 16), 2 * rows)
        mid = fw // 2
        for n in range(2):
            part = [v[n * rows : (n + 1) * rows, :] for v in pair]
            ref[j, here, n * mid : (n + 1) * mid] = jnp.concatenate(part, axis=0).astype(BF)

    def hidden(h):
        @pl.loop(0, 4 * NF)
        def _(i):
            j, k = i // 4, i % 4
            pair = []
            for n in range(2):
                g = act[h, 2 * j, 2 * k + n].astype(F32)
                u = act[h, 2 * j + 1, 2 * k + n].astype(F32)
                pair.append(g * jax.nn.sigmoid(g) * u)
            unfold_store(hid, h, j, k, pair)

    def gate_backward(h, j):
        @pl.loop(0, 4)
        def _(k):
            gates, ups = [], []
            for n in range(2):
                g = act[h, 2 * j, 2 * k + n].astype(F32)
                u = act[h, 2 * j + 1, 2 * k + n].astype(F32)
                d = dh[h, j, 2 * k + n].astype(F32)
                sig = jax.nn.sigmoid(g)
                gates.append(d * u * sig * (1.0 + g * (1.0 - sig)))
                ups.append(d * g * sig)
            unfold_store(dact, h, 2 * j, k, gates)
            unfold_store(dact, h, 2 * j + 1, k, ups)

    def half_copy(h, d):
        return remote(
            half_out.at[h, d], half_in.at[h, d], h_send.at[h, d], h_recv.at[h, d], at.sibling()
        )

    def unpack(h, d, core):
        value = term[h, d, :, :dw]
        high = value.astype(BF)
        low = (value - high.astype(F32)).astype(BF)
        back = p_back[pl.ds(pl.multiple_of(core * 256, 256), 256), :]
        return dot(back, high) + dot(back, low)

    def parts(h):
        here = half_rows(h)
        if h == 0:
            for copy in weights[1:]:
                copy.wait()

        def arrived(j):
            for node in reversed(SPREAD[h].leaves):
                ag_arrive(h, j, node)
            gate_backward(h, j)

        def part(j, d):
            units = pl.ds(pl.multiple_of(d * dw, dw), dw)
            value = dot_nt(dact[2 * j, here, :], wg[j, units, :])
            return value + dot_nt(dact[2 * j + 1, here, :], wu[j, units, :])

        for j in range(NF - 1):
            arrived(j)

            @pl.loop(0, ND)
            def _(d):
                value = part(j, d)
                term[h, d, :, :dw] = value + term[h, d, :, :dw] if j else value

        arrived(NF - 1)

        @pl.loop(0, ND)
        def _(d):
            term[h, d, :, :dw] = term[h, d, :, :dw] + part(NF - 1, d)
            half_out[h, d] = unpack(h, d, 1 - at.core).astype(BF)
            half_copy(h, d).start()

    def mp_chunk(h, d, offset):
        owner = at.chip_at(-offset[0], offset[1])
        return term[h, d, pl.ds(pl.multiple_of(owner * 32, 32), 32), :dw]

    def mp_copy(h, d, node):
        e = HOME[h].index(node)
        return remote(
            mp_out.at[h, d, e],
            mp_in.at[h, d, e],
            m_send.at[h, d, e],
            m_recv.at[h, d, e],
            at.mp_hop(node, HOME[h].to[node]),
        )

    def mp_sum(h, d, node):
        value = mp_chunk(h, d, node)
        for child in HOME[h].children(node):
            e = HOME[h].index(child)
            arrival(mp_in.at[h, d, e], m_send.at[h, d, e], m_recv.at[h, d, e], at)
            value = value + mp_in[h, d, e].astype(F32)
        return value

    def mp_hop(h, d, node):
        mp_out[h, d, HOME[h].index(node)] = mp_sum(h, d, node).astype(BF)
        mp_copy(h, d, node).start()

    def mp_leaves(h):
        @pl.loop(0, ND)
        def _(d):
            value = unpack(h, d, at.core)
            half_copy(h, d).wait_recv()
            term[h, d, :256, :dw] = value + half_in[h, d].astype(F32)
            for node in HOME[h].leaves:
                mp_hop(h, d, node)

    def mp_inner(h):
        if HOME[h].inner:

            @pl.loop(0, ND)
            def _(d):
                for node in HOME[h].inner:
                    mp_hop(h, d, node)

    def mp_own(h):
        sums = [mp_sum(h, d, (0, 0)) for d in range(ND)]
        for k in range(4):
            both = jnp.concatenate([s[k * 8 : k * 8 + 8, :] for s in sums], axis=0)
            fin_out[2 * k + ((at.core + h) & 1)] = both.astype(BF)

    def tn(a, b):
        return lax.dot_general(a, b, (((0,), (0,)), ((), ())), preferred_element_type=F32).astype(BF)

    def weight_grad(j):
        for n, out in enumerate((gg_out, gu_out)):
            out[:, piece(j)] = tn(dyc[...], dact[2 * j + n])

    def down_grads():
        @pl.loop(0, NF)
        def _(j):
            gd_out[piece(j), :] = tn(hid[j], dyc[...])

    a, b = 0, 1
    one_hot(p_slab, a, a, True)
    one_hot(p_own, 0, a, False)
    pack(a, 0)
    gather_dy[b].start(slab_of(rbuf, b))
    for copy in weights[1:]:
        copy.start()
    pack(a, 1)
    one_hot(p_slab, b, b, True)
    back_matrix(a)
    for level in range(1, DY_TREE[a].levels + 1):
        gather_dy[a].relay(level)
    gather_dy[b].relay(1)
    gather_dy[a].finish()
    terms(a)
    for level in range(2, DY_TREE[b].levels + 1):
        gather_dy[b].relay(level)
    one_hot(p_own, 0, b, False)
    rs_inner(a, 0)
    gather_dy[b].finish()
    rs_inner(a, 1)
    terms(b)
    rs_inner(a, 2)
    pack(b, 0)
    rs_own(a)
    rs_inner(b, 0)
    from_dp(rbuf_x, ax_send, ax_recv)
    for h in range(2):
        gather_x[h].start(slab_of(rbuf_x, h))
    rs_inner(b, 1)
    pack(b, 1)
    rs_inner(b, 2)
    hidden(a)
    ag_forward(a, 1)
    hidden(b)
    rs_own(b)
    down_grads()
    ag_forward(a, 2)
    for h in range(2):
        gather_x[h].relay(1)
    ag_forward(b, 1)
    parts(a)
    ag_forward(b, 2)
    for h in range(2):
        gather_x[h].relay(2)
    mp_leaves(a)
    back_matrix(b)
    parts(b)
    mp_inner(a)
    mp_leaves(b)
    for h in range(2):
        gather_x[h].finish()
        dyc[half_rows(h), :] = dot(p_slab[h], xb[h]).astype(BF)
    mp_own(a)

    def weight_grads(first, last):
        @pl.loop(first, last)
        def _(j):
            weight_grad(j)

    mp_inner(b)
    weight_grads(0, 1)
    mp_own(b)
    to_dp(fin_out, fin_in, f_send, f_recv)
    weight_grads(1, NF)
    for gather in gather_dy + gather_x:
        gather.drain()

    for h in range(2):

        @pl.loop(0, NF)
        def _(j):
            for node in STAR.nodes:
                rs_copy(h, j, node).wait_send()
                ag_copy(h, j, node).wait_send()

        @pl.loop(0, ND)
        def _(d):
            half_copy(h, d).wait_send()
            for node in STAR.nodes:
                mp_copy(h, d, node).wait_send()

    from_dp(fin_in, f_send, f_recv)
    for c in range(8):
        both = fin_in[c].astype(F32)
        for d in range(ND):
            gt_out[:, c * dl + d * dw : c * dl + (d + 1) * dw] = both[d * 8 : d * 8 + 8, :].astype(BF)
    for copy in sent:
        copy.wait_send()


def main_call(size, number, tokens, out_grad, gate_pre, up_pre, wg, wu, wd, lengths):
    dl, fl = tokens.shape[1] // 8, gate_pre.shape[1]
    fw, dw, cap, rows = fl // NF, dl // ND, size // 2, size // 16
    dma = pltpu.SemaphoreType.DMA
    vmem, smem = pl.BlockSpec(memory_space=pltpu.VMEM), pl.BlockSpec(memory_space=pltpu.SMEM)
    anywhere = pl.BlockSpec(memory_space=pl.ANY)
    buffers = [
        (tokens.shape, BF),
        (tokens.shape, BF),
        ((8, 16, dw + 128), BF),
        ((8, 16, dw + 128), BF),
        ((8, 16, dw), BF),
        ((8, 16, dw), BF),
        ((2, 512, dl), BF),
        ((2, 512, dl), BF),
        ((2, cap, 512), BF),
        ((1, cap, 1024), BF),
        ((512, cap), BF),
        ((size, dl), BF),
        ((NF, dl, fw), BF),
        ((NF, dl, fw), BF),
        ((2, 2 * NF, 8, 2 * rows, fw // 2), BF),
        ((NF, size, fw), BF),
        ((2 * NF, size, fw), BF),
        ((2, NF, cap, fw), F32),
        ((2, NF, 7, 2 * rows, fw // 2), BF),
        ((2, NF, 7, 2 * rows, fw // 2), BF),
        ((2, NF, 8, 2 * rows, fw // 2), BF),
        ((2, ND, 256, dw), BF),
        ((2, ND, 256, dw), BF),
        ((2, ND, 7, 32, dw), BF),
        ((2, ND, 7, 32, dw), BF),
        ((8, 16, dw), BF),
        ((8, 16, dw), BF),
    ]
    sems = [(2,), (8,), (8,), (8,), (8,), (1 + 2 * NF,), (2,)]
    sems += [(2, NF, 7)] * 4
    sems += [(2, 7), (2, 7), (2, 8), (2, 8)] * 2
    sems += [(2, ND), (2, ND), (2, ND, 7), (2, ND, 7), (8,), (8,)]
    return pl.pallas_call(
        main_kernel,
        out_shape=(
            jax.ShapeDtypeStruct((8, dl * 8), BF),
            jax.ShapeDtypeStruct((dl, fl), BF),
            jax.ShapeDtypeStruct((dl, fl), BF),
            jax.ShapeDtypeStruct((fl, dl), BF),
            jax.ShapeDtypeStruct((1,), jnp.int32),
        ),
        in_specs=[anywhere, anywhere, smem] + [anywhere] * 5,
        out_specs=(vmem,) * 4 + (smem,),
        scratch_shapes=[pltpu.VMEM(s, t) for s, t in buffers] + [dma(s) for s in sems],
        compiler_params=pltpu.CompilerParams(
            collective_id=number, has_side_effects=True, vmem_limit_bytes=(38 if size <= SIZE else 63) * MIB
        ),
    )(tokens, out_grad, lengths, gate_pre, up_pre, wg, wu, wd)


def copy_kernel(*refs):
    sem, refs = refs[-1], refs[:-1]
    count = len(refs) // 2
    copies = [
        pltpu.make_async_copy(refs[n], refs[count + n], sem.at[n]) for n in range(count)
    ]
    for copy in copies:
        copy.start()
    for copy in copies:
        copy.wait()


def copy_out(arrays):
    anywhere = pl.BlockSpec(memory_space=pl.ANY)
    return pl.pallas_call(
        copy_kernel,
        out_shape=tuple(jax.ShapeDtypeStruct(a.shape, a.dtype) for a in arrays),
        in_specs=[pl.BlockSpec(memory_space=pltpu.VMEM)] * len(arrays),
        out_specs=(anywhere,) * len(arrays),
        scratch_shapes=[pltpu.SemaphoreType.DMA((len(arrays),))],
        compiler_params=pltpu.CompilerParams(vmem_limit_bytes=24 * MIB),
    )(*arrays)


def local(*args):
    *outs, over = main_call(SIZE, 0, *args)

    def again(state):
        *full, _ = main_call(1024, 1, *args)
        return (jnp.int32(0), *copy_out(full))

    state = (over[0], *copy_out(outs))
    return lax.while_loop(lambda state: state[0] > 0, again, state)[1:]


def solution(mesh):
    in_specs = (
        P(("dp", "mp"), None),
        P(("dp", "mp"), None),
        P(None, "mp"),
        P(None, "mp"),
        P("dp", "mp"),
        P("dp", "mp"),
        P("mp", "dp"),
        P("dp"),
    )
    out_specs = (P(("dp", "mp"), None), P("dp", "mp"), P("dp", "mp"), P("mp", "dp"))
    return jax.shard_map(local, mesh=mesh, in_specs=in_specs, out_specs=out_specs, check_vma=False)
```
